32 devices in a mesh: row: 4 (over z), col: 8 (over y, x, core).
Axes of the slice: x: 2, y: 2, z: 4, core: 2. Of those that a mesh axis runs over, the one named last changes fastest.
Arguments:
- pair: bfloat16 [256, 256, 128], P('row', 'col'), may hold values from -24 to 24
- token_mask: int32 [256], replicated, may hold values 0 or 1
- ln_gain: float32 [128], replicated, may hold values from 0.5 to 1.5
- ln_shift: float32 [128], replicated, may hold values from -3 to 3
- w_qkv: bfloat16 [128, 384], replicated, may hold values from -1 to 1
- w_bias: bfloat16 [128, 4], replicated, may hold values from -12 to 12
- w_gate: bfloat16 [128, 128], replicated, may hold values from -0.5 to 0.5
- gate_bias: float32 [128], replicated, may hold values from -4 to 4
- w_out: bfloat16 [128, 128], replicated, may hold values from -0.5 to 0.5
- out_bias: float32 [128], replicated, may hold values from -3 to 3
Outputs:
- update: bfloat16 [256, 256, 128], P('row', 'col')
The draws below stay inside these ranges and needn't reach their ends.
All inputs are finite; a program needn't handle non-finite values.
Results may differ from the reference program's by a relative error of at most 0.001.
The reference program's roundings to bfloat16 on the way (of `normed`, `bias`, `weights`, `attended` and `gated`) count: a program that leaves them out, or rounds other values in their place, can miss the bound.
Values may be sent and summed in bfloat16 or wider, within the bound.
No kernel may reach another device: no remote copies, remote signals or barrier semaphores. Data moves between devices by JAX's collectives and lax.ppermute only.
A program may use at most 192 MiB of HBM per device.

```python
import math
import jax
import jax.numpy as jnp
from jax import lax

C = 128
HD = 32
H = 4
N = 256


def draw_pair(key, part):
    key = jax.random.fold_in(key, 7)
    first = jax.random.fold_in(key, 0)
    values = jnp.clip(jax.random.normal(first, (N, N, C), jnp.float32), -6.0, 6.0)
    return values.astype(jnp.bfloat16)


def draw_w_bias(key, part):
    key = jax.random.fold_in(key, 13)
    values = jax.random.normal(key, (C, H), jnp.float32) * C ** (-0.5)
    return jnp.clip(values, -12.0, 12.0).astype(jnp.bfloat16)


def draw_w_qkv(key, part):
    key = jax.random.fold_in(key, 19)
    first = jax.random.fold_in(key, 0)
    values = jax.random.normal(first, (C, 3 * H * HD), jnp.float32) * C ** (-0.5)
    return jnp.clip(values, -1.0, 1.0).astype(jnp.bfloat16)


def touch_ends(result, stream_key, least, top_value):
    longest = result.shape.index(max(result.shape))
    spots = []
    for shift in (0, 1):
        where = [jax.random.randint(jax.random.fold_in(stream_key, axis), (), 0, length) for axis, length in enumerate(result.shape)]
        where[longest] = (where[longest] + shift) % result.shape[longest]
        spots.append(tuple(where))
    return result.at[spots[0]].set(least).at[spots[1]].set(top_value)


def gaussian(key, shape, width, bound, kind=jnp.bfloat16):
    result = jax.random.normal(key, shape, jnp.float32) * width
    return jnp.minimum(jnp.maximum(result, -bound), bound).astype(kind)


def setup_inputs(seed: int = 0) -> dict:
    arg_keys = jax.random.split(jax.random.key(seed), 11)
    return {
        "pair": draw_pair(jax.random.fold_in(arg_keys[10], 71), 0),
        "token_mask": touch_ends((jax.random.randint(arg_keys[1], (N,), 0, 8) < 7).astype(jnp.int32), jax.random.fold_in(arg_keys[1], 1), 0, 1),
        "ln_gain": jnp.clip(1.0 + 0.1 * jax.random.normal(arg_keys[2], (C,), jnp.float32), 0.5, 1.5),
        "ln_shift": gaussian(arg_keys[3], (C,), 0.5, 3.0, jnp.float32),
        "w_qkv": draw_w_qkv(jax.random.fold_in(arg_keys[10], 71), 0),
        "w_bias": draw_w_bias(jax.random.fold_in(arg_keys[10], 71), 0),
        "w_gate": gaussian(arg_keys[6], (C, H * HD), C ** -0.5, 0.5),
        "gate_bias": gaussian(arg_keys[7], (H * HD,), 1.0, 4.0, jnp.float32),
        "w_out": gaussian(arg_keys[8], (H * HD, C), (H * HD) ** -0.5, 0.5),
        "out_bias": gaussian(arg_keys[9], (C,), 0.5, 3.0, jnp.float32),
    }


def layer_norm(pair, ln_gain, ln_shift):
    values = pair.astype(jnp.float32)
    mean = lax.optimization_barrier(jnp.mean(values, -1, keepdims=True))
    centred = values - mean
    var = lax.optimization_barrier(jnp.mean(centred * centred, -1, keepdims=True))
    return (centred * lax.rsqrt(var + 1e-05) * ln_gain + ln_shift).astype(jnp.bfloat16)

def reference(pair, token_mask, ln_gain, ln_shift, w_qkv, w_bias, w_gate, gate_bias, w_out, out_bias):
    count = pair.shape[0]
    chans = pair.shape[2]
    heads = w_bias.shape[1]
    inner = w_gate.shape[1]
    head = inner // heads
    normed = layer_norm(pair, ln_gain, ln_shift).reshape(count * count, chans)
    mixed = jnp.dot(normed, w_qkv, preferred_element_type=jnp.float32)
    qscale = jnp.where(jnp.arange(3 * inner) < inner, head ** (-0.5), 1.0).astype(jnp.float32)
    qkv = (mixed * qscale).astype(jnp.bfloat16).reshape(count, count, 3, heads, head)
    bias = jnp.dot(normed, w_bias, preferred_element_type=jnp.float32).astype(jnp.bfloat16).reshape(count, count, heads)
    gate = jax.nn.sigmoid(jnp.dot(normed, w_gate, preferred_element_type=jnp.float32) + gate_bias)
    bias_t = bias.transpose(2, 1, 0).astype(jnp.float32)
    key_bias = jnp.where(token_mask == 1, 0.0, -1000000000.0).astype(jnp.float32)
    block = math.gcd(count, 8)

    def column_block(start):
        piece = lax.dynamic_slice_in_dim(qkv, start, block, 1).astype(jnp.float32)
        query = piece[:, :, 0]
        keys = piece[:, :, 1]
        vals = piece[:, :, 2]
        scores = jnp.einsum('ajhd,kjhd->hajk', query, keys) + bias_t[:, :, None, :] + key_bias
        top = lax.optimization_barrier(jnp.max(scores, -1, keepdims=True))
        expo = jnp.exp(scores - top)
        weights = (expo / lax.optimization_barrier(jnp.sum(expo, -1, keepdims=True))).astype(jnp.bfloat16)
        return jnp.einsum('hajk,kjhd->ajhd', weights.astype(jnp.float32), vals).astype(jnp.bfloat16)
    starts = (jnp.arange(count // block) * block).astype(jnp.int32)
    blocks = lax.map(column_block, starts)
    attended = blocks.transpose(1, 0, 2, 3, 4).reshape(count * count, inner)
    gated = (gate * attended.astype(jnp.float32)).astype(jnp.bfloat16)
    update = jnp.dot(gated, w_out, preferred_element_type=jnp.float32) + out_bias
    return update.astype(jnp.bfloat16).reshape(count, count, chans)
```

```python
import functools

import jax
import jax.numpy as jnp
from jax import lax
from jax.experimental import pallas as pl
from jax.experimental.pallas import tpu as pltpu
from jax.sharding import PartitionSpec as P

BF = jnp.bfloat16
F32 = jnp.float32
VMEM_LIMIT = 52 * 1024 * 1024


def dot(a, b):
    return jnp.dot(a, b, preferred_element_type=F32)


def dot_t(a, b):
    return lax.dot_general(a, b, (((1,), (1,)), ((), ())), preferred_element_type=F32)


def transposed(a):
    return a.astype(F32).T.astype(BF)


def column_of(row, width):
    return jnp.broadcast_to(row, (width, row.shape[1])).T


def split_sum(a, ones):
    first = a.astype(BF)
    rest = a - first.astype(F32)
    second = rest.astype(BF)
    third = (rest - second.astype(F32)).astype(BF)
    return dot(first, ones) + dot(second, ones) + dot(third, ones)


def prep_kernel(pair_ref, gain_ref, shift_ref, wb_ref, *refs):
    chunks, tile_ref, wide = refs[:-2], refs[-2], refs[-1]
    rows, cols, chans = pair_ref.shape
    heads = wb_ref.shape[0]
    lanes = heads * cols
    parts = len(chunks)
    width = cols // parts
    me = lax.axis_index("row")
    ones = jnp.ones((chans, chans), BF)
    head_of = lax.broadcasted_iota(jnp.int32, (lanes, heads), 0) // cols
    spread = (head_of == lax.broadcasted_iota(jnp.int32, (lanes, heads), 1)).astype(BF)
    wb = dot(spread, wb_ref[...]).astype(BF)
    lane_col = lax.broadcasted_iota(jnp.int32, (cols, lanes), 1) % cols
    keep = lane_col == lax.broadcasted_iota(jnp.int32, (cols, lanes), 0)
    gain = gain_ref[...]
    shift = shift_ref[...]
    step = min(rows, 16)

    def body(index, carry):
        start = pl.multiple_of(index * step, step)
        raw = pair_ref[pl.ds(start, step)].reshape(step * cols, chans)
        mean = dot(raw, ones) * (1.0 / chans)
        centred = raw.astype(F32) - mean
        var = split_sum(centred * centred, ones) * (1.0 / chans)
        normed = (centred * lax.rsqrt(var + 1e-05) * gain + shift).astype(BF)
        wide[pl.ds(pl.multiple_of(index * step * cols, step * cols), step * cols), :] = normed.astype(F32)
        every = dot_t(normed, wb).reshape(step, cols, lanes)
        tile = jnp.sum(jnp.where(keep[None], every, 0.0), axis=1)
        tile_ref[pl.ds(start, step), :] = tile.astype(BF)
        return carry

    lax.fori_loop(0, rows // step, body, 0)
    for s in range(parts):
        first = (me ^ s) * width
        for j in range(width):
            chunks[s][j] = wide[pl.ds(first + j, rows, stride=cols), :].astype(BF)


def attend_kernel(parts, *refs):
    pieces = refs[:parts]
    bias_a, bias_b, mask_ref, wqkv_ref, wg_ref, gb_ref, wo_ref, ob_ref = refs[parts : parts + 8]
    outs = refs[parts + 8 : 2 * parts + 8]
    normed, update, tiles, bias, key_bias, wt, queries, keys, vals, heard, gates, sem_p, sem_b, sem_o = refs[2 * parts + 8 :]
    width, rows, chans = pieces[0].shape
    pairs, _, _, lanes = bias_a.shape
    heads = bias.shape[0]
    count = bias.shape[1]
    cols = lanes // heads
    inner = wg_ref.shape[1]
    head = inner // heads
    me = lax.axis_index("row")
    col = lax.axis_index("col")

    bias_copies = []
    for k, source in enumerate((bias_a, bias_b)):
        for t in range(pairs):
            copy = pltpu.make_async_copy(
                source.at[t], tiles.at[col ^ (2 * t + k)], sem_b.at[k * pairs + t]
            )
            copy.start()
            bias_copies.append(copy)
    piece_copies = []
    for s in range(parts):
        copy = pltpu.make_async_copy(pieces[s], normed.at[me ^ s], sem_p.at[s])
        copy.start()
        piece_copies.append(copy)

    wt[0:inner] = transposed(wqkv_ref[:, 2 * inner : 3 * inner])
    wt[inner : 2 * inner] = transposed(wg_ref[...])
    wt[2 * inner : 2 * inner + chans] = transposed(wo_ref[...])
    gate_bias = column_of(gb_ref[...], 128)[:, 0:1]
    out_bias = column_of(ob_ref[...], 128)[:, 0:1]
    key_bias[...] = jnp.where(column_of(mask_ref[...], 128) == 1, 0.0, -1000000000.0).astype(F32)

    for copy in bias_copies:
        copy.wait()
    group = 128 // cols
    span = group * lanes
    source_lane = lax.broadcasted_iota(jnp.int32, (span, span), 0)
    target_lane = lax.broadcasted_iota(jnp.int32, (span, span), 1)
    tile_of, rest = source_lane // lanes, source_lane % lanes
    wanted = (rest // cols) * 128 + tile_of * cols + rest % cols
    order = (wanted == target_lane).astype(BF)
    groups = count // 128

    batch = max(1, min(count, 256) // rows)

    def one_block(index, carry):
        g, b = index // (parts // batch), index % (parts // batch)
        block = jnp.concatenate(
            [
                tiles[g * group + t, pl.ds(b * batch, batch)].reshape(batch * rows, lanes)
                for t in range(group)
            ],
            axis=1,
        )
        ordered = dot(block, order)
        across = pl.ds(pl.multiple_of(g * 128, 128), 128)
        for s in range(batch):
            at = pl.ds(pl.multiple_of((me ^ (b * batch + s)) * rows, rows), rows)
            for h in range(heads):
                bias[h, at, across] = (
                    ordered[s * rows : (s + 1) * rows, h * 128 : (h + 1) * 128] + key_bias[at, :]
                )
        return carry

    blocks = groups * (parts // batch)
    lax.fori_loop(0, blocks, one_block, 0, unroll=blocks <= 2)

    for copy in piece_copies:
        copy.wait()
    lane_head = lax.broadcasted_iota(jnp.int32, (1, inner), 1) // head
    wide = heard.shape[1]

    def one_column(j, carry):
        tokens = normed[:, j].reshape(count, chans)
        mixed = dot(tokens, wqkv_ref[:, 0 : 2 * inner])
        query = (mixed[:, 0:inner] * (head ** (-0.5))).astype(BF)
        keys[...] = mixed[:, inner : 2 * inner].astype(BF)
        vals_gate = dot_t(wt[0 : 2 * inner], tokens)
        vals[...] = vals_gate[0:inner].astype(BF)
        queries[...] = query
        gates[...] = jax.nn.sigmoid(vals_gate[inner : 2 * inner] + gate_bias)

        def one_part(g, inside):
            lo = pl.multiple_of(g * wide, wide)
            some = queries[pl.ds(lo, wide), :]

            def one_head(h, within):
                at = pl.ds(pl.multiple_of(h * head, head), head)
                head_keys = jnp.where(lane_head == h, keys[...], jnp.zeros_like(keys))
                scores = dot_t(head_keys, some) + bias[h, :, pl.ds(lo, wide)]
                top = jnp.max(scores, axis=0, keepdims=True)
                expo = jnp.exp(scores - top)
                total = jnp.sum(expo, axis=0, keepdims=True)
                weights = (expo * (1.0 / total)).astype(BF)
                heard[at, :] = dot(vals[at, :], weights)
                return within

            lax.fori_loop(0, heads, one_head, 0, unroll=count == wide)
            attended = heard[...].astype(BF).astype(F32)
            gated = (gates[:, pl.ds(lo, wide)] * attended).astype(BF)
            result = dot(wt[2 * inner : 2 * inner + chans], gated) + out_bias
            result = result.T.astype(BF)
            for p in range(wide // rows):
                update[g * (wide // rows) + p, j] = result[p * rows : (p + 1) * rows]
            return inside

        lax.fori_loop(0, count // wide, one_part, 0, unroll=count == wide)
        return carry

    lax.fori_loop(0, width, one_column, 0)
    out_copies = []
    for s in range(parts):
        copy = pltpu.make_async_copy(update.at[me ^ s], outs[s], sem_o.at[s])
        copy.start()
        out_copies.append(copy)
    for copy in out_copies:
        copy.wait()


def place_kernel(*refs):
    pieces, out_ref, wide = refs[:-2], refs[-2], refs[-1]
    rows, cols, chans = out_ref.shape
    width = cols // len(pieces)
    me = lax.axis_index("row")
    for s, piece in enumerate(pieces):
        first = (me ^ s) * width

        def one_column(j, carry, first=first, piece=piece):
            wide[pl.ds(first + j, rows, stride=cols), :] = piece[j].astype(F32)
            return carry

        lax.fori_loop(0, width, one_column, 0, unroll=rows <= 64)
    step = min(rows, 16)

    def body(index, carry):
        lines = wide[pl.ds(pl.multiple_of(index * step * cols, step * cols), step * cols), :]
        out_ref[pl.ds(index * step, step)] = lines.astype(BF).reshape(step, cols, chans)
        return carry

    lax.fori_loop(0, rows // step, body, 0)


def per_device(
    pair, token_mask, ln_gain, ln_shift, w_qkv, w_bias, w_gate, gate_bias, w_out, out_bias
):
    rows, cols, chans = pair.shape
    heads = w_bias.shape[1]
    inner = w_gate.shape[1]
    parts = lax.axis_size("row")
    col_count = lax.axis_size("col")
    count = rows * parts
    width = cols // parts
    lanes = heads * cols
    lane_part = 256 if count <= 256 else 128
    chunk = jax.ShapeDtypeStruct((width, rows, chans), BF)
    vmem = pl.BlockSpec(memory_space=pltpu.VMEM)
    anywhere = pl.BlockSpec(memory_space=pl.ANY)
    params = pltpu.CompilerParams(vmem_limit_bytes=VMEM_LIMIT)

    def swap(x, axis, offset):
        size = lax.axis_size(axis)
        return lax.ppermute(x, axis, [(i, i ^ offset) for i in range(size)])

    *chunks, tile = pl.pallas_call(
        prep_kernel,
        out_shape=[chunk] * parts + [jax.ShapeDtypeStruct((rows, lanes), BF)],
        in_specs=[vmem] * 4,
        out_specs=[vmem] * (parts + 1),
        scratch_shapes=[pltpu.VMEM((rows * cols, chans), F32)],
        compiler_params=params,
        name="prep",
    )(pair, ln_gain.reshape(1, chans), ln_shift.reshape(1, chans), w_bias.T)

    by_row = jnp.stack([tile] + [swap(tile, "row", s) for s in range(1, parts)])
    pieces = [chunks[0]] + [swap(chunks[s], "row", s) for s in range(1, parts)]
    by_chip = jnp.stack([by_row] + [swap(by_row, "col", 2 * t) for t in range(1, col_count // 2)])
    other = swap(by_chip, "col", 1)

    returned = pl.pallas_call(
        functools.partial(attend_kernel, parts),
        out_shape=[chunk] * parts,
        in_specs=[anywhere] * (parts + 2) + [vmem] * 6,
        out_specs=[anywhere] * parts,
        scratch_shapes=[
            pltpu.VMEM((parts, width, rows, chans), BF),
            pltpu.VMEM((parts, width, rows, chans), BF),
            pltpu.VMEM((col_count, parts, rows, lanes), BF),
            pltpu.VMEM((heads, count, count), F32),
            pltpu.VMEM((count, 128), F32),
            pltpu.VMEM((2 * inner + chans, chans), BF),
            pltpu.VMEM((count, inner), BF),
            pltpu.VMEM((count, inner), BF),
            pltpu.VMEM((inner, count), BF),
            pltpu.VMEM((inner, lane_part), F32),
            pltpu.VMEM((inner, count), F32),
            pltpu.SemaphoreType.DMA((parts,)),
            pltpu.SemaphoreType.DMA((col_count,)),
            pltpu.SemaphoreType.DMA((parts,)),
        ],
        compiler_params=params,
        name="attend",
    )(
        *pieces,
        by_chip,
        other,
        token_mask.reshape(1, count),
        w_qkv,
        w_gate,
        gate_bias.reshape(1, inner),
        w_out,
        out_bias.reshape(1, chans),
    )
    back = [returned[0]] + [swap(returned[s], "row", s) for s in range(1, parts)]
    return pl.pallas_call(
        place_kernel,
        out_shape=jax.ShapeDtypeStruct((rows, cols, chans), BF),
        in_specs=[vmem] * parts,
        out_specs=vmem,
        scratch_shapes=[pltpu.VMEM((rows * cols, chans), F32)],
        compiler_params=params,
        name="place",
    )(*back)


def solution(mesh):
    in_specs = (P("row", "col", None), P(), P(), P(), P(), P(), P(), P(), P(), P())
    out_specs = P("row", "col", None)
    return jax.shard_map(
        per_device, mesh=mesh, in_specs=in_specs, out_specs=out_specs, check_vma=False
    )
```

```python
import functools

import jax
import jax.numpy as jnp
from jax import lax
from jax.experimental import pallas as pl
from jax.experimental.pallas import tpu as pltpu
from jax.sharding import PartitionSpec as P

BF = jnp.bfloat16
F32 = jnp.float32
VMEM_LIMIT = 52 * 1024 * 1024
VMEM_ALONE = 62 * 1024 * 1024


def dot(a, b):
    return jnp.dot(a, b, preferred_element_type=F32)


def dot_t(a, b):
    return lax.dot_general(a, b, (((1,), (1,)), ((), ())), preferred_element_type=F32)


def dot_l(a, b):
    return lax.dot_general(a, b, (((0,), (0,)), ((), ())), preferred_element_type=F32)


def over(a, size):
    return lax.shift_right_logical(a, jnp.full_like(a, size.bit_length() - 1))


def below(a, size):
    return a & (size - 1)


def column_of(row, width):
    return jnp.broadcast_to(row, (width, row.shape[1])).T


def split_sum(a, ones):
    first = a.astype(BF)
    rest = a - first.astype(F32)
    second = rest.astype(BF)
    third = (rest - second.astype(F32)).astype(BF)
    return dot(first, ones) + dot(second, ones) + dot(third, ones)


def prep_kernel(pair_ref, gain_ref, shift_ref, wb_ref, *refs):
    parcels, (raw, gain, shift, wbt, wide, sem) = refs[:-6], refs[-6:]
    rows, cols, chans = pair_ref.shape
    heads = wb_ref.shape[0]
    lanes = heads * cols
    parts = len(parcels)
    width = cols // parts
    me = lax.axis_index("row")
    step = wide.shape[0]
    small = [
        pltpu.make_async_copy(source, target, sem.at[n])
        for n, (source, target) in enumerate(((wb_ref, wbt), (gain_ref, gain), (shift_ref, shift)))
    ]
    for copy in small:
        copy.start()

    half = rows // 2
    fetches = [
        pltpu.make_async_copy(
            pair_ref.at[pl.ds(n * half, half)], raw.at[pl.ds(n * half, half)], sem.at[3 + n]
        )
        for n in range(2)
    ]
    for copy in fetches:
        copy.start()
    ones = jnp.ones((chans, chans), BF)
    lane_col = below(lax.broadcasted_iota(jnp.int32, (cols, lanes), 1), cols)
    keep = lane_col == lax.broadcasted_iota(jnp.int32, (cols, lanes), 0)
    head_of = over(lax.broadcasted_iota(jnp.int32, (lanes, heads), 0), cols)
    spread = (head_of == lax.broadcasted_iota(jnp.int32, (lanes, heads), 1)).astype(BF)
    for copy in small:
        copy.wait()
    wb = dot(spread, wbt[...]).astype(BF)

    def body(index, carry):
        start = pl.multiple_of(index * step, step)
        values = raw[pl.ds(start, step)].reshape(step * cols, chans)
        mean = dot(values, ones) * (1.0 / chans)
        centred = values.astype(F32) - mean
        var = split_sum(centred * centred, ones) * (1.0 / chans)
        normed = (centred * lax.rsqrt(var + 1e-05) * gain[...] + shift[...]).astype(BF)
        every = dot_t(normed, wb).reshape(step, cols, lanes)
        tile = jnp.sum(jnp.where(keep[None], every, 0.0), axis=1).astype(BF)
        wide[...] = normed.astype(F32).reshape(step, cols, chans)
        to = pl.ds(pl.multiple_of(start * width, step * width), step * width)
        for s in range(parts):
            first = pl.multiple_of((me ^ s) * width, width)
            chunk = wide[:, pl.ds(first, width), :].reshape(step * width, chans)
            parcels[s][to, :] = chunk.astype(BF)
            for n in range(lanes // chans):
                row = pl.multiple_of(rows * (width + n) + start, step)
                parcels[s][pl.ds(row, step), :] = tile[:, n * chans : (n + 1) * chans]
        return carry

    for n in range(2):
        fetches[n].wait()
        lax.fori_loop(n * half // step, (n + 1) * half // step, body, 0, unroll=rows <= 64)


def project_kernel(parts, scale, rows, width, offset, *refs):
    parcels = refs[:parts]
    wqkv_ref, wg_ref, gb_ref, q_ref, k_ref, v_ref, gate_ref = refs[parts : parts + 7]
    wide, tokens, weight, gate_bias, sem = refs[parts + 7 :]
    some, count, inner = q_ref.shape
    me = lax.axis_index("row")
    copies = [
        pltpu.make_async_copy(wqkv_ref, weight.at[:, pl.ds(0, 3 * inner)], sem.at[0]),
        pltpu.make_async_copy(wg_ref, weight.at[:, pl.ds(3 * inner, inner)], sem.at[1]),
        pltpu.make_async_copy(gb_ref, gate_bias, sem.at[2]),
    ]
    for copy in copies:
        copy.start()
    for s in range(parts):
        wide[s] = parcels[s][0 : rows * width, :].astype(F32)
    for copy in copies:
        copy.wait()

    def one_column(j, carry):
        for s in range(parts):
            at = pl.ds(pl.multiple_of((me ^ s) * rows, rows), rows)
            tokens[at, :] = wide[s, pl.ds(offset + j, rows, stride=width), :].astype(BF)
        mixed = dot(tokens[...], weight[...])
        q_ref[j] = (mixed[:, 0:inner] * scale).astype(BF)
        k_ref[j] = mixed[:, inner : 2 * inner].astype(BF)
        v_ref[j] = mixed[:, 2 * inner : 3 * inner].astype(BF)
        gate_ref[j] = jax.nn.sigmoid(mixed[:, 3 * inner : 4 * inner] + gate_bias[...])
        return carry

    lax.fori_loop(0, some, one_column, 0, unroll=2)


def attend_kernel(parts, *refs):
    halves = refs[0:4], refs[4:8]
    bias_a, bias_b, mask_ref, wo_ref, ob_ref = refs[8:13]
    outs = refs[13 : parts + 13]
    update, tiles, bias, key_bias, heard, mask, out_weight, out_bias, sem = refs[parts + 13 :]
    part, count, inner = halves[0][0].shape
    width = 2 * part
    pairs, _, layers, rows, chans = bias_a.shape
    heads = bias.shape[0]
    lanes = layers * chans
    cols = lanes // heads
    head = inner // heads
    me = lax.axis_index("row")
    col = lax.axis_index("col")
    copies = [
        pltpu.make_async_copy(source, target, sem.at[n])
        for n, (source, target) in enumerate(
            ((mask_ref, mask), (wo_ref, out_weight), (ob_ref, out_bias))
        )
    ]
    for copy in copies:
        copy.start()
    for k, source in enumerate((bias_a, bias_b)):
        for t in range(pairs):
            tiles[col ^ (2 * t + k)] = source[t]

    group = 128 // cols
    span = group * lanes
    source_lane = lax.broadcasted_iota(jnp.int32, (span, span), 0)
    target_lane = lax.broadcasted_iota(jnp.int32, (span, span), 1)
    tile_of, rest = over(source_lane, lanes), below(source_lane, lanes)
    wanted = over(rest, cols) * 128 + tile_of * cols + below(rest, cols)
    order = (wanted == target_lane).astype(BF)
    batch = max(1, min(count, 256) // rows)
    for copy in copies:
        copy.wait()
    key_bias[...] = jnp.where(column_of(mask[...], 128) == 1, 0.0, -1000000000.0).astype(F32)

    def one_block(index, carry):
        g, b = index // (parts // batch), index % (parts // batch)
        block = jnp.concatenate(
            [
                tiles[g * group + t, pl.ds(b * batch, batch), n].reshape(batch * rows, chans)
                for t in range(group)
                for n in range(layers)
            ],
            axis=1,
        )
        ordered = dot(block, order)
        across = pl.ds(pl.multiple_of(g * 128, 128), 128)
        for s in range(batch):
            at = pl.ds(pl.multiple_of((me ^ (b * batch + s)) * rows, rows), rows)
            for h in range(heads):
                bias[h, at, across] = (
                    ordered[s * rows : (s + 1) * rows, h * 128 : (h + 1) * 128] + key_bias[at, :]
                )
        return carry

    blocks = (count // 128) * (parts // batch)
    lax.fori_loop(0, blocks, one_block, 0, unroll=blocks <= 2)

    lane_head = over(lax.broadcasted_iota(jnp.int32, (1, inner), 1), head)
    wide = heard.shape[0]

    def one_column(half, j, carry):
        q_ref, k_ref, v_ref, gate_ref = halves[half]

        def one_part(g, inside):
            at = pl.ds(pl.multiple_of(g * wide, wide), wide)
            some = q_ref[j, at, :]
            heard[...] = jnp.zeros_like(heard)

            def one_head(h, within):
                mine = lane_head == h
                head_keys = jnp.where(mine, k_ref[j], jnp.zeros((count, inner), BF))
                head_vals = jnp.where(mine, v_ref[j], jnp.zeros((count, inner), BF))
                scores = dot_t(head_keys, some) + bias[h, :, at]
                top = jnp.max(scores, axis=0, keepdims=True)
                expo = jnp.exp(scores - top)
                total = jnp.sum(expo, axis=0, keepdims=True)
                weights = (expo * (1.0 / total)).astype(BF)
                heard[...] += dot_l(weights, head_vals)
                return within

            lax.fori_loop(0, heads, one_head, 0, unroll=count == wide)
            attended = heard[...].astype(BF).astype(F32)
            gated = (gate_ref[j, at, :] * attended).astype(BF)
            result = dot(gated, out_weight[...]) + out_bias[...]
            update[pl.ds(g * wide * width + half * part + j, wide, stride=width), :] = result
            return inside

        lax.fori_loop(0, count // wide, one_part, 0, unroll=count == wide)
        return carry

    for half in range(2):
        body = functools.partial(one_column, half)
        lax.fori_loop(0, part, body, 0, unroll=part if count == wide else 1)
    for s in range(parts):
        at = pl.ds(pl.multiple_of((me ^ s) * rows * width, rows * width), rows * width)
        outs[s][...] = update[at, :].astype(BF).reshape(rows, width, chans)


def place_kernel(*refs):
    pieces, out_ref, wide = refs[:-2], refs[-2], refs[-1]
    rows, cols, chans = out_ref.shape
    width = cols // len(pieces)
    me = lax.axis_index("row")
    step = wide.shape[0]

    def body(index, carry):
        at = pl.ds(pl.multiple_of(index * step, step), step)
        for s, piece in enumerate(pieces):
            first = pl.multiple_of((me ^ s) * width, width)
            wide[:, pl.ds(first, width), :] = piece[at].astype(F32)
        out_ref[at] = wide[...].astype(BF)
        return carry

    lax.fori_loop(0, rows // step, body, 0, unroll=rows <= 64)


def per_device(
    pair, token_mask, ln_gain, ln_shift, w_qkv, w_bias, w_gate, gate_bias, w_out, out_bias
):
    rows, cols, chans = pair.shape
    heads = w_bias.shape[1]
    inner = w_gate.shape[1]
    parts = lax.axis_size("row")
    col_count = lax.axis_size("col")
    count = rows * parts
    width = cols // parts
    lanes = heads * cols
    lane_part = 256 if count <= 256 else 128
    chunk = jax.ShapeDtypeStruct((rows, width, chans), BF)
    vmem = pl.BlockSpec(memory_space=pltpu.VMEM)
    hbm = pl.BlockSpec(memory_space=pltpu.HBM)
    large = count > 256
    params = pltpu.CompilerParams(vmem_limit_bytes=VMEM_LIMIT if large else VMEM_LIMIT // 4)
    alone = pltpu.CompilerParams(vmem_limit_bytes=VMEM_ALONE)

    def swap(x, axis, offset):
        size = lax.axis_size(axis)
        return lax.ppermute(x, axis, [(i, i ^ offset) for i in range(size)])

    layers = lanes // chans
    step = min(rows, 16)
    parcels = pl.pallas_call(
        prep_kernel,
        out_shape=[jax.ShapeDtypeStruct((rows * (width + layers), chans), BF)] * parts,
        in_specs=[hbm] * 4,
        out_specs=[vmem] * parts,
        scratch_shapes=[
            pltpu.VMEM((rows, cols, chans), BF),
            pltpu.VMEM((1, chans), F32),
            pltpu.VMEM((1, chans), F32),
            pltpu.VMEM((heads, chans), BF),
            pltpu.VMEM((step, cols, chans), F32),
            pltpu.SemaphoreType.DMA((5,)),
        ],
        compiler_params=alone,
        name="prep",
    )(pair, ln_gain.reshape(1, chans), ln_shift.reshape(1, chans), w_bias.T)

    parcels = [parcels[0]] + [swap(parcels[s], "row", s) for s in range(1, parts)]
    by_row = jnp.stack([p[rows * width :].reshape(layers, rows, chans) for p in parcels])
    by_chip = jnp.stack([by_row] + [swap(by_row, "col", 2 * t) for t in range(1, col_count // 2)])
    part = width // 2

    def project(offset):
        return pl.pallas_call(
            functools.partial(
                project_kernel, parts, (inner // heads) ** (-0.5), rows, width, offset
            ),
            out_shape=[jax.ShapeDtypeStruct((part, count, inner), BF)] * 3
            + [jax.ShapeDtypeStruct((part, count, inner), F32)],
            in_specs=[vmem] * parts + [hbm] * 3,
            out_specs=[vmem] * 4,
            scratch_shapes=[
                pltpu.VMEM((parts, rows * width, chans), F32),
                pltpu.VMEM((count, chans), BF),
                pltpu.VMEM((chans, 4 * inner), BF),
                pltpu.VMEM((1, inner), F32),
                pltpu.SemaphoreType.DMA((3,)),
            ],
            cost_estimate=pl.CostEstimate(
                flops=8 * part * count * chans * inner,
                bytes_accessed=part * count * (2 * chans + 10 * inner),
                transcendentals=part * count * inner,
            ),
            compiler_params=params,
            name="project",
        )(*parcels, w_qkv, w_gate, gate_bias.reshape(1, inner))

    first = project(0)
    by_chip, first = lax.optimization_barrier((by_chip, first))
    other = swap(by_chip, "col", 1)
    second = project(part)

    returned = pl.pallas_call(
        functools.partial(attend_kernel, parts),
        out_shape=[chunk] * parts,
        in_specs=[vmem] * 10 + [hbm] * 3,
        out_specs=[vmem] * parts,
        scratch_shapes=[
            pltpu.VMEM((count * width, chans), F32),
            pltpu.VMEM((col_count, parts, layers, rows, chans), BF),
            pltpu.VMEM((heads, count, count), F32),
            pltpu.VMEM((count, 128), F32),
            pltpu.VMEM((lane_part, inner), F32),
            pltpu.VMEM((1, count), jnp.int32),
            pltpu.VMEM((inner, chans), BF),
            pltpu.VMEM((1, chans), F32),
            pltpu.SemaphoreType.DMA((3,)),
        ],
        cost_estimate=pl.CostEstimate(
            flops=8 * width * count * count * inner,
            bytes_accessed=width * count * 12 * inner,
            transcendentals=width * heads * count * count,
        ),
        compiler_params=params,
        name="attend",
    )(
        *first,
        *second,
        by_chip,
        other,
        token_mask.reshape(1, count),
        w_out,
        out_bias.reshape(1, chans),
    )
    back = [returned[0]] + [swap(returned[s], "row", s) for s in range(1, parts)]
    return pl.pallas_call(
        place_kernel,
        out_shape=jax.ShapeDtypeStruct((rows, cols, chans), BF),
        in_specs=[vmem] * parts,
        out_specs=vmem,
        scratch_shapes=[pltpu.VMEM((min(rows, 16), cols, chans), F32)],
        compiler_params=params,
        name="place",
    )(*back)


def solution(mesh):
    in_specs = (P("row", "col", None), P(), P(), P(), P(), P(), P(), P(), P(), P())
    out_specs = P("row", "col", None)
    return jax.shard_map(
        per_device, mesh=mesh, in_specs=in_specs, out_specs=out_specs, check_vma=False
    )
```

```python
import functools

import jax
import jax.numpy as jnp
from jax import lax
from jax.experimental import pallas as pl
from jax.experimental.pallas import tpu as pltpu
from jax.sharding import PartitionSpec as P

BF = jnp.bfloat16
F32 = jnp.float32
VMEM_LIMIT = 52 * 1024 * 1024
VMEM_ALONE = 62 * 1024 * 1024


def dot(a, b):
    return jnp.dot(a, b, preferred_element_type=F32)


def dot_t(a, b):
    return lax.dot_general(a, b, (((1,), (1,)), ((), ())), preferred_element_type=F32)


def dot_l(a, b):
    return lax.dot_general(a, b, (((0,), (0,)), ((), ())), preferred_element_type=F32)


def over(a, size):
    return lax.shift_right_logical(a, jnp.full_like(a, size.bit_length() - 1))


def below(a, size):
    return a & (size - 1)


def hop(s, parts):
    return (parts - s) % parts


def column_of(row, width):
    return jnp.broadcast_to(row, (width, row.shape[1])).T


def split_sum(a, ones):
    first = a.astype(BF)
    rest = a - first.astype(F32)
    second = rest.astype(BF)
    third = (rest - second.astype(F32)).astype(BF)
    return dot(first, ones) + dot(second, ones) + dot(third, ones)


def prep_kernel(pair_ref, gain_ref, shift_ref, wb_ref, *refs):
    parcels, (raw, gain, shift, wbt, wide, sem) = refs[:-6], refs[-6:]
    parts = len(parcels) // 2
    rows, cols, chans = pair_ref.shape
    heads = wb_ref.shape[0]
    lanes = heads * cols
    width = cols // parts
    me = lax.axis_index("row")
    step = wide.shape[0]
    half = rows // 2
    small = [
        pltpu.make_async_copy(source, target, sem.at[n])
        for n, (source, target) in enumerate(((wb_ref, wbt), (gain_ref, gain), (shift_ref, shift)))
    ]
    for copy in small:
        copy.start()

    fetches = [
        pltpu.make_async_copy(
            pair_ref.at[pl.ds(n * half, half)], raw.at[pl.ds(n * half, half)], sem.at[3 + n]
        )
        for n in range(2)
    ]
    for copy in fetches:
        copy.start()
    ones = jnp.ones((chans, chans), BF)
    lane_col = below(lax.broadcasted_iota(jnp.int32, (cols, lanes), 1), cols)
    keep = lane_col == lax.broadcasted_iota(jnp.int32, (cols, lanes), 0)
    head_of = over(lax.broadcasted_iota(jnp.int32, (lanes, heads), 0), cols)
    spread = (head_of == lax.broadcasted_iota(jnp.int32, (lanes, heads), 1)).astype(BF)
    for copy in small:
        copy.wait()
    wb = dot(spread, wbt[...]).astype(BF)

    def body(n, index, carry):
        start = pl.multiple_of(n * half + index * step, step)
        values = raw[pl.ds(start, step)].reshape(step * cols, chans)
        mean = dot(values, ones) * (1.0 / chans)
        centred = values.astype(F32) - mean
        var = split_sum(centred * centred, ones) * (1.0 / chans)
        normed = (centred * lax.rsqrt(var + 1e-05) * gain[...] + shift[...]).astype(BF)
        every = dot_t(normed, wb).reshape(step, cols, lanes)
        tile = jnp.sum(jnp.where(keep[None], every, 0.0), axis=1).astype(BF)
        wide[...] = normed.astype(F32).reshape(step, cols, chans)
        to = pl.ds(pl.multiple_of(index * (step * width), step * width), step * width)
        for s in range(parts):
            first = pl.multiple_of((me ^ hop(s, parts)) * width, width)
            chunk = wide[:, pl.ds(first, width), :].reshape(step * width, chans)
            parcels[n * parts + s][to, :] = chunk.astype(BF)
            for layer in range(lanes // chans):
                row = pl.multiple_of(half * width + rows * layer + start, step)
                parcels[s][pl.ds(row, step), :] = tile[:, layer * chans : (layer + 1) * chans]
        return carry

    for n in range(2):
        fetches[n].wait()
        lax.fori_loop(0, half // step, functools.partial(body, n), 0, unroll=rows <= 64)


def project_kernel(parts, scale, half, *refs):
    parcels = refs[:parts]
    weight, gate_bias, q_ref, k_ref, v_ref, gate_ref, wide, tokens = refs[parts:]
    width, count, inner = q_ref.shape
    me = lax.axis_index("row")
    for s in range(parts):
        wide[s] = parcels[s][0 : half * width, :].astype(F32)

    def two_columns(j, carry):
        for k in range(2):
            for s in range(parts):
                at = pl.multiple_of(k * count + (me ^ hop(s, parts)) * half, half)
                line = wide[s, pl.ds(2 * j + k, half, stride=width), :]
                tokens[pl.ds(at, half), :] = line.astype(BF)
        mixed = dot(tokens[...], weight[...])
        query = (mixed[:, 0:inner] * scale).astype(BF)
        gate = jax.nn.sigmoid(mixed[:, 3 * inner : 4 * inner] + gate_bias[...])
        for k in range(2):
            at = slice(k * count, (k + 1) * count)
            q_ref[2 * j + k] = query[at]
            k_ref[2 * j + k] = mixed[at, inner : 2 * inner].astype(BF)
            v_ref[2 * j + k] = mixed[at, 2 * inner : 3 * inner].astype(BF)
            gate_ref[2 * j + k] = gate[at]
        return carry

    lax.fori_loop(0, width // 2, two_columns, 0, unroll=2 if half <= 32 else 1)


def constants_kernel(parts, cols, lanes, *refs):
    mask_ref, wqkv_ref, wg_ref, gb_ref, wo_ref, ob_ref = refs[:6]
    weight_ref, gate_ref, out_ref, base_ref, order_ref, key_ref, mask, scratch, sem = refs[6:]
    inner = wg_ref.shape[1]
    moves = (
        (mask_ref, mask),
        (wqkv_ref, weight_ref.at[:, pl.ds(0, 3 * inner)]),
        (wg_ref, weight_ref.at[:, pl.ds(3 * inner, inner)]),
        (gb_ref, gate_ref),
        (wo_ref, out_ref),
        (ob_ref, base_ref),
    )
    copies = [
        pltpu.make_async_copy(source, target, sem.at[n])
        for n, (source, target) in enumerate(moves)
    ]
    for copy in copies:
        copy.start()
    span = order_ref.shape[0]
    source_lane = lax.broadcasted_iota(jnp.int32, (span, span), 0)
    target_lane = lax.broadcasted_iota(jnp.int32, (span, span), 1)
    tile_of, rest = over(source_lane, lanes), below(source_lane, lanes)
    wanted = over(rest, cols) * 128 + tile_of * cols + below(rest, cols)
    order_ref[...] = (wanted == target_lane).astype(BF)
    for copy in copies:
        copy.wait()
    scratch[...] = jnp.where(column_of(mask[...], 128) == 1, 0.0, -1000000000.0).astype(F32)
    count = key_ref.shape[0]
    half = count // parts // 2
    for n in range(2):
        for p in range(parts):
            key_ref[(n * parts + p) * half : (n * parts + p + 1) * half] = scratch[
                (2 * p + n) * half : (2 * p + n + 1) * half
            ]


def attend_kernel(parts, side, *refs):
    halves = refs[0:4], refs[4:8]
    tiles, out_weight, out_bias, order_ref, key_ref = refs[8:13]
    outs = refs[13 : parts + 13]
    update, bias = refs[parts + 13 :]
    width, half, inner = halves[0][0].shape
    count = 2 * half
    pairs, _, layers, rows, chans = tiles.shape
    groups = bias.shape[0]
    heads = bias.shape[2] // 128
    lanes = layers * chans
    cols = lanes // heads
    head = inner // heads
    me = lax.axis_index("row")
    col = lax.axis_index("col")
    group = 128 // cols
    batch = max(1, min(count, 256) // rows)

    def one_block(index, carry):
        g, b = index // (parts // batch), index % (parts // batch)
        block = jnp.concatenate(
            [
                tiles[g * group + t, pl.ds(b * batch, batch), n].reshape(batch * rows, chans)
                for t in range(group)
                for n in range(layers)
            ],
            axis=1,
        )
        ordered = dot(block, order_ref[...])
        for s in range(batch):
            for n in range(2):
                at = n * half + (me ^ hop(b * batch + s, parts)) * cols
                at = pl.ds(pl.multiple_of(at, cols), cols)
                low = s * rows + n * cols
                for h in range(heads):
                    across = slice(h * 128, (h + 1) * 128)
                    bias[g, at, across] = ordered[low : low + cols, across] + key_ref[at, :]
        return carry

    blocks = groups * (parts // batch)
    lax.fori_loop(0, blocks, one_block, 0, unroll=blocks <= 2)

    lane_head = over(lax.broadcasted_iota(jnp.int32, (1, inner), 1), head)
    odd = (col & 1) ^ side

    def one_column(j, carry):
        keys = jnp.concatenate([halves[0][1][j], halves[1][1][j]], axis=0)
        vals = jnp.concatenate([halves[0][2][j], halves[1][2][j]], axis=0)

        def one_group(g, inside):
            places = [
                pl.ds(pl.multiple_of((over(col, 2) ^ (g * group + t)) * cols, cols), cols)
                for t in range(group)
            ]

            def gathered(n):
                both = [
                    jnp.concatenate([halves[k][n][j, at, :] for at in places], axis=0)
                    for k in range(2)
                ]
                return jnp.where(odd == 1, both[1], both[0])

            query = gathered(0)
            gate = gathered(3)
            blank = jnp.zeros_like(query)
            attended = jnp.zeros((128, inner), F32)
            for h in range(0, heads, 2):
                some = jnp.concatenate(
                    [jnp.where(lane_head == n, query, blank) for n in (h, h + 1)], axis=0
                )
                scores = dot_t(keys, some) + bias[g, :, h * 128 : (h + 2) * 128]
                top = jnp.max(scores, axis=0, keepdims=True)
                expo = jnp.exp(scores - top)
                total = jnp.sum(expo, axis=0, keepdims=True)
                weights = (expo * (1.0 / total)).astype(BF)
                heard = dot_l(weights, vals)
                attended = jnp.where(lane_head == h, heard[0:128], attended)
                attended = jnp.where(lane_head == h + 1, heard[128:256], attended)
            gated = (gate * attended.astype(BF).astype(F32)).astype(BF)
            result = dot(gated, out_weight[...]) + out_bias[...]
            update[pl.ds(g * 128 * width + j, 128, stride=width), :] = result
            return inside

        lax.fori_loop(0, groups, one_group, 0, unroll=groups == 1)
        return carry

    lax.fori_loop(0, width, one_column, 0, unroll=width if groups == 1 else 1)
    for s in range(parts):
        at = (hop(s, parts) ^ me ^ over(col, 2)) * (cols * width)
        at = pl.ds(pl.multiple_of(at, cols * width), cols * width)
        outs[s][...] = update[at, :].astype(BF).reshape(cols, width, chans)


def place_kernel(parts, *refs):
    out_ref, wide = refs[2 * parts :]
    rows, cols, chans = out_ref.shape
    width = cols // parts
    me = lax.axis_index("row")
    odd = lax.axis_index("col") & 1
    step = wide.shape[1]

    def body(index, carry):
        for side in range(2):
            for s in range(parts):
                first = pl.multiple_of((me ^ hop(s, parts)) * width, width)
                at = pl.ds(pl.multiple_of(index * step, step), step)
                wide[side, :, pl.ds(first, width), :] = refs[side * parts + s][at].astype(F32)
            at = pl.multiple_of((odd ^ side) * (rows // 2) + index * step, step)
            out_ref[pl.ds(at, step)] = wide[side].astype(BF)
        return carry

    lax.fori_loop(0, rows // 2 // step, body, 0, unroll=rows <= 64)


def per_device(
    pair, token_mask, ln_gain, ln_shift, w_qkv, w_bias, w_gate, gate_bias, w_out, out_bias
):
    rows, cols, chans = pair.shape
    heads = w_bias.shape[1]
    inner = w_gate.shape[1]
    parts = lax.axis_size("row")
    col_count = lax.axis_size("col")
    count = rows * parts
    width = cols // parts
    lanes = heads * cols
    vmem = pl.BlockSpec(memory_space=pltpu.VMEM)
    hbm = pl.BlockSpec(memory_space=pltpu.HBM)
    large = count > 256
    params = pltpu.CompilerParams(vmem_limit_bytes=VMEM_LIMIT if large else VMEM_LIMIT // 4)
    alone = pltpu.CompilerParams(vmem_limit_bytes=VMEM_ALONE)

    def swap(x, axis, offset):
        size = lax.axis_size(axis)
        return lax.ppermute(x, axis, [(i, i ^ offset) for i in range(size)])

    layers = lanes // chans
    step = min(rows, 16)
    half = rows // 2
    parcels = pl.pallas_call(
        prep_kernel,
        out_shape=[jax.ShapeDtypeStruct((half * width + rows * layers, chans), BF)] * parts
        + [jax.ShapeDtypeStruct((half * width, chans), BF)] * parts,
        in_specs=[hbm] * 4,
        out_specs=[vmem] * (2 * parts),
        scratch_shapes=[
            pltpu.VMEM((rows, cols, chans), BF),
            pltpu.VMEM((1, chans), F32),
            pltpu.VMEM((1, chans), F32),
            pltpu.VMEM((heads, chans), BF),
            pltpu.VMEM((step, cols, chans), F32),
            pltpu.SemaphoreType.DMA((5,)),
        ],
        compiler_params=alone,
        name="prep",
    )(pair, ln_gain.reshape(1, chans), ln_shift.reshape(1, chans), w_bias.T)

    span = (128 // cols) * lanes
    shared = pl.pallas_call(
        functools.partial(constants_kernel, parts, cols, lanes),
        out_shape=[
            jax.ShapeDtypeStruct((chans, 4 * inner), BF),
            jax.ShapeDtypeStruct((1, inner), F32),
            jax.ShapeDtypeStruct((inner, chans), BF),
            jax.ShapeDtypeStruct((1, chans), F32),
            jax.ShapeDtypeStruct((span, span), BF),
            jax.ShapeDtypeStruct((count, 128), F32),
        ],
        in_specs=[hbm] * 6,
        out_specs=[vmem] * 6,
        scratch_shapes=[
            pltpu.VMEM((1, count), jnp.int32),
            pltpu.VMEM((count, 128), F32),
            pltpu.SemaphoreType.DMA((6,)),
        ],
        cost_estimate=pl.CostEstimate(
            flops=span * span * 8, bytes_accessed=span * span * 2, transcendentals=0
        ),
        compiler_params=params,
        name="constants",
    )(
        token_mask.reshape(1, count),
        w_qkv,
        w_gate,
        gate_bias.reshape(1, inner),
        w_out,
        out_bias.reshape(1, chans),
    )

    def back(pieces):
        return [pieces[0]] + [swap(pieces[s], "row", hop(s, parts)) for s in range(1, parts)]

    early = back(parcels[:parts])
    shared, *waiting = lax.optimization_barrier((shared, *parcels[parts:]))
    late = back(waiting)

    def project(pieces):
        return pl.pallas_call(
            functools.partial(project_kernel, parts, (inner // heads) ** (-0.5), half),
            out_shape=[jax.ShapeDtypeStruct((width, count // 2, inner), BF)] * 3
            + [jax.ShapeDtypeStruct((width, count // 2, inner), F32)],
            in_specs=[vmem] * (parts + 2),
            out_specs=[vmem] * 4,
            scratch_shapes=[
                pltpu.VMEM((parts, half * width, chans), F32),
                pltpu.VMEM((count, chans), BF),
            ],
            cost_estimate=pl.CostEstimate(
                flops=4 * width * count * chans * inner,
                bytes_accessed=width * count * (chans + 5 * inner),
                transcendentals=width * count * inner // 2,
            ),
            compiler_params=params,
            name="project",
        )(*pieces, weight, gate_row)

    by_row = jnp.stack([p[half * width :].reshape(layers, rows, chans) for p in early])
    weight, gate_row, *shared = shared
    from_chips = [swap(by_row, "col", 2 * t) for t in range(1, col_count // 2)]
    first = project(early)
    second = project(late)
    from_chips, second = lax.optimization_barrier((from_chips, second))
    by_chip = jnp.stack([by_row] + from_chips)
    other = swap(by_chip, "col", 1)

    block = jax.ShapeDtypeStruct((cols, width, chans), BF)

    def attend(side, tiles):
        return pl.pallas_call(
            functools.partial(attend_kernel, parts, side),
            out_shape=[block] * parts,
            in_specs=[vmem] * 13,
            out_specs=[vmem] * parts,
            scratch_shapes=[
                pltpu.VMEM((count // 2 * width, chans), F32),
                pltpu.VMEM((count // 256, count, heads * 128), F32),
            ],
            cost_estimate=pl.CostEstimate(
                flops=4 * width * count * count * inner,
                bytes_accessed=width * count * 8 * inner,
                transcendentals=width * heads * count * count // 2,
            ),
            compiler_params=params,
            name="attend",
        )(*first, *second, tiles, *shared)

    same = back(attend(0, by_chip))
    crossed = back(attend(1, other))
    return pl.pallas_call(
        functools.partial(place_kernel, parts),
        out_shape=jax.ShapeDtypeStruct((rows, cols, chans), BF),
        in_specs=[vmem] * (2 * parts),
        out_specs=vmem,
        scratch_shapes=[pltpu.VMEM((2, min(rows // 2, 16), cols, chans), F32)],
        compiler_params=params,
        name="place",
    )(*same, *crossed)


def solution(mesh):
    in_specs = (P("row", "col", None), P(), P(), P(), P(), P(), P(), P(), P(), P())
    out_specs = P("row", "col", None)
    return jax.shard_map(
        per_device, mesh=mesh, in_specs=in_specs, out_specs=out_specs, check_vma=False
    )
```

```python
import functools

import jax
import jax.numpy as jnp
from jax import lax
from jax.experimental import pallas as pl
from jax.experimental.pallas import tpu as pltpu
from jax.sharding import PartitionSpec as P

BF = jnp.bfloat16
F32 = jnp.float32
VMEM_LIMIT = 52 * 1024 * 1024
VMEM_ALONE = 62 * 1024 * 1024


def dot(a, b):
    return jnp.dot(a, b, preferred_element_type=F32)


def dot_t(a, b):
    return lax.dot_general(a, b, (((1,), (1,)), ((), ())), preferred_element_type=F32)


def dot_l(a, b):
    return lax.dot_general(a, b, (((0,), (0,)), ((), ())), preferred_element_type=F32)


def over(a, size):
    return lax.shift_right_logical(a, jnp.full_like(a, size.bit_length() - 1))


def below(a, size):
    return a & (size - 1)


def hop(s, parts):
    return (parts - s) % parts


def column_of(row, width):
    return jnp.broadcast_to(row, (width, row.shape[1])).T


def split_sum(a, ones):
    first = a.astype(BF)
    rest = a - first.astype(F32)
    second = rest.astype(BF)
    third = (rest - second.astype(F32)).astype(BF)
    return dot(first, ones) + dot(second, ones) + dot(third, ones)


def pipelined(count, stages, lags):
    kept = {}
    for turn in range(count + max(lags)):
        for k, (stage, lag) in enumerate(zip(stages, lags)):
            if 0 <= turn - lag < count:
                given = kept.pop((k - 1, turn - lag), ())
                kept[k, turn - lag] = stage(turn - lag, *given)


def prep_kernel(pair_ref, gain_ref, shift_ref, wb_ref, *refs):
    parcels, (raw, gain, shift, wbt, wide, sem) = refs[:-6], refs[-6:]
    parts = len(parcels) // 2
    rows, cols, chans = pair_ref.shape
    heads = wb_ref.shape[0]
    lanes = heads * cols
    width = cols // parts
    me = lax.axis_index("row")
    step = min(rows, 16)
    half = rows // 2
    first_rows = rows // 4
    small = [
        pltpu.make_async_copy(source, target, sem.at[n])
        for n, (source, target) in enumerate(((wb_ref, wbt), (gain_ref, gain), (shift_ref, shift)))
    ]
    for copy in small:
        copy.start()

    fetches = [
        pltpu.make_async_copy(
            pair_ref.at[pl.ds(n * half, half)], raw.at[pl.ds(n * half, half)], sem.at[3 + n]
        )
        for n in range(2)
    ]
    for copy in fetches:
        copy.start()
    ones = jnp.ones((chans, chans), BF)
    lane_col = below(lax.broadcasted_iota(jnp.int32, (cols, lanes), 1), cols)
    keep = lane_col == lax.broadcasted_iota(jnp.int32, (cols, lanes), 0)
    head_of = over(lax.broadcasted_iota(jnp.int32, (lanes, heads), 0), cols)
    spread = (head_of == lax.broadcasted_iota(jnp.int32, (lanes, heads), 1)).astype(BF)
    for copy in small:
        copy.wait()
    wb = dot(spread, wbt[...]).astype(BF)

    def centre(start):
        values = raw[pl.ds(start, step)].reshape(step * cols, chans)
        mean = dot(values, ones) * (1.0 / chans)
        centred = values.astype(F32) - mean
        return centred, split_sum(centred * centred, ones) * (1.0 / chans)

    def scale(start, centred, var):
        normed = (centred * lax.rsqrt(var + 1e-05) * gain[...] + shift[...]).astype(BF)
        return normed, dot_t(normed, wb)

    def store(start, which, normed, every):
        every = every.reshape(step, cols, lanes)
        tile = jnp.sum(jnp.where(keep[None], every, 0.0), axis=1).astype(BF)
        wide[pl.ds(start, step)] = normed.astype(F32).reshape(step, cols, chans)
        to = pl.multiple_of((start - which * first_rows) * width, step * width)
        to = pl.ds(to, step * width)
        for s in range(parts):
            first = pl.multiple_of((me ^ hop(s, parts)) * width, width)
            chunk = wide[pl.ds(start, step), pl.ds(first, width), :].reshape(step * width, chans)
            parcels[which * parts + s][to, :] = chunk.astype(BF)
            for layer in range(lanes // chans):
                row = pl.multiple_of(first_rows * width + rows * layer + start, step)
                parcels[s][pl.ds(row, step), :] = tile[:, layer * chans : (layer + 1) * chans]
        return ()

    if rows <= 64:

        def first_stage(n):
            if n * step in (0, half):
                fetches[n * step // half].wait()
            return centre(n * step)

        def second_stage(n, centred, var):
            return scale(n * step, centred, var)

        def third_stage(n, normed, every):
            return store(n * step, int(n * step >= first_rows), normed, every)

        pipelined(rows // step, (first_stage, second_stage, third_stage), (0, 1, 2))
    else:
        for copy in fetches:
            copy.wait()
        for low, high, which in ((0, first_rows, 0), (first_rows, rows, 1)):

            def one(index, carry, low=low, which=which):
                start = pl.multiple_of(low + index * step, step)
                store(start, which, *scale(start, *centre(start)))
                return carry

            lax.fori_loop(0, (high - low) // step, one, 0)


def project_kernel(parts, scale, size, *refs):
    parcels = refs[:parts]
    weight, gate_bias, q_ref, k_ref, v_ref, gate_ref, wide, tokens = refs[parts:]
    width, count, inner = q_ref.shape
    batch = tokens.shape[1] // count
    me = lax.axis_index("row")
    for s in range(parts):
        wide[s] = parcels[s][0 : size * width, :].astype(F32)

    def lay(j):
        for k in range(batch):
            for s in range(parts):
                at = pl.multiple_of(k * count + (me ^ hop(s, parts)) * size, size)
                line = wide[s, pl.ds(batch * j + k, size, stride=width), :]
                tokens[j, pl.ds(at, size), :] = line.astype(BF)
        return ()

    def multiply(j):
        return (dot(tokens[j], weight[...]),)

    def store(j, mixed):
        query = (mixed[:, 0:inner] * scale).astype(BF)
        gate = jax.nn.sigmoid(mixed[:, 3 * inner : 4 * inner] + gate_bias[...])
        for k in range(batch):
            at = slice(k * count, (k + 1) * count)
            q_ref[batch * j + k] = query[at]
            k_ref[batch * j + k] = mixed[at, inner : 2 * inner].astype(BF)
            v_ref[batch * j + k] = mixed[at, 2 * inner : 3 * inner].astype(BF)
            gate_ref[batch * j + k] = gate[at]
        return ()

    if count <= 256:
        pipelined(width // batch, (lay, multiply, store), (0, 1, 2))
    else:

        def one(j, carry):
            lay(j)
            store(j, *multiply(j))
            return carry

        lax.fori_loop(0, width // batch, one, 0)


def constants_kernel(parts, cols, lanes, *refs):
    mask_ref, wqkv_ref, wg_ref, gb_ref, wo_ref, ob_ref = refs[:6]
    weight_ref, gate_ref, out_ref, base_ref, order_ref, key_ref, mask, scratch, sem = refs[6:]
    inner = wg_ref.shape[1]
    moves = (
        (mask_ref, mask),
        (wqkv_ref, weight_ref.at[:, pl.ds(0, 3 * inner)]),
        (wg_ref, weight_ref.at[:, pl.ds(3 * inner, inner)]),
        (gb_ref, gate_ref),
        (wo_ref, out_ref),
        (ob_ref, base_ref),
    )
    copies = [
        pltpu.make_async_copy(source, target, sem.at[n])
        for n, (source, target) in enumerate(moves)
    ]
    for copy in copies:
        copy.start()
    span = order_ref.shape[0]
    source_lane = lax.broadcasted_iota(jnp.int32, (span, span), 0)
    target_lane = lax.broadcasted_iota(jnp.int32, (span, span), 1)
    tile_of, rest = over(source_lane, lanes), below(source_lane, lanes)
    wanted = over(rest, cols) * 128 + tile_of * cols + below(rest, cols)
    order_ref[...] = (wanted == target_lane).astype(BF)
    for copy in copies:
        copy.wait()
    scratch[...] = jnp.where(column_of(mask[...], 128) == 1, 0.0, -1000000000.0).astype(F32)
    rows = key_ref.shape[0] // parts
    first_rows = rows // 4
    to = 0
    for low, high in ((0, first_rows), (first_rows, rows)):
        for p in range(parts):
            key_ref[to : to + high - low] = scratch[p * rows + low : p * rows + high]
            to += high - low


def attend_kernel(parts, side, *refs):
    halves = refs[0:4], refs[4:8]
    tiles, out_weight, out_bias, order_ref, key_ref = refs[8:13]
    outs = refs[13 : parts + 13]
    update, bias = refs[parts + 13 :]
    width, early, inner = halves[0][0].shape
    count = early + halves[1][0].shape[1]
    first_rows = early // parts
    pairs, _, layers, rows, chans = tiles.shape
    groups = bias.shape[0]
    heads = bias.shape[2] // 128
    lanes = layers * chans
    cols = lanes // heads
    head = inner // heads
    me = lax.axis_index("row")
    col = lax.axis_index("col")
    group = 128 // cols
    batch = max(1, min(count, 256) // rows)

    def one_block(index, carry):
        g, b = index // (parts // batch), index % (parts // batch)
        block = jnp.concatenate(
            [
                tiles[g * group + t, pl.ds(b * batch, batch), n].reshape(batch * rows, chans)
                for t in range(group)
                for n in range(layers)
            ],
            axis=1,
        )
        ordered = dot(block, order_ref[...])
        for s in range(batch):
            level = me ^ hop(b * batch + s, parts)
            for low, high, base in ((0, first_rows, 0), (first_rows, rows, early)):
                at = pl.multiple_of(base + level * (high - low), first_rows)
                at = pl.ds(at, high - low)
                some = slice(s * rows + low, s * rows + high)
                for h in range(heads):
                    across = slice(h * 128, (h + 1) * 128)
                    bias[g, at, across] = ordered[some, across] + key_ref[at, :]
        return carry

    blocks = groups * (parts // batch)
    lax.fori_loop(0, blocks, one_block, 0, unroll=blocks <= 2)

    lane_head = over(lax.broadcasted_iota(jnp.int32, (1, inner), 1), head)
    odd = (col & 1) ^ side

    def query_rows(j, g, n):
        found = []
        for t in range(group):
            level = over(col, 2) ^ (g * group + t)
            base = level * (rows - first_rows)
            spots = (0, level * first_rows), (1, base + first_rows), (1, base + odd * 2 * first_rows)
            upper, lower, last = (
                halves[k][n][j, pl.ds(pl.multiple_of(at, first_rows), first_rows), :]
                for k, at in spots
            )
            found += [jnp.where(odd == 1, lower, upper), last]
        return jnp.concatenate(found, axis=0)

    def key_rows(j, n):
        return jnp.concatenate([halves[0][n][j], halves[1][n][j]], axis=0)

    def scores_of(j, g, h):
        query = query_rows(j, g, 0)
        blank = jnp.zeros_like(query)
        pair = [jnp.where(lane_head == n, query, blank) for n in (h, h + 1)]
        product = dot_t(key_rows(j, 1), jnp.concatenate(pair, axis=0))
        return product + bias[g, :, h * 128 : (h + 2) * 128]

    def weights_of(scores):
        top = jnp.max(scores, axis=0, keepdims=True)
        expo = jnp.exp(scores - top)
        total = jnp.sum(expo, axis=0, keepdims=True)
        return (expo * (1.0 / total)).astype(BF)

    def finish(j, g, heard):
        attended = jnp.zeros((128, inner), F32)
        for n in range(heads):
            part = heard[n // 2][n % 2 * 128 : (n % 2 + 1) * 128]
            attended = jnp.where(lane_head == n, part, attended)
        gated = (query_rows(j, g, 3) * attended.astype(BF).astype(F32)).astype(BF)
        result = dot(gated, out_weight[...]) + out_bias[...]
        update[pl.ds(g * 128 * width + j, 128, stride=width), :] = result

    def several(columns, g):
        steps = [(j, h) for j in columns for h in range(0, heads, 2)]
        scores = scores_of(steps[0][0], g, steps[0][1])
        total_steps = len(steps)
        scores, weights, heard = {}, {}, {}
        for n in range(-3, total_steps + 2 + 2):
            if 0 <= n + 3 < total_steps:
                j, h = steps[n + 3]
                scores[n + 3] = scores_of(j, g, h)
            if 0 <= n < total_steps:
                weights[n] = weights_of(scores.pop(n))
            k = n - 2
            if 0 <= k < total_steps:
                heard[k] = dot_l(weights.pop(k), key_rows(steps[k][0], 2))
            k = n - 2 - 2
            if 0 <= k < total_steps and steps[k][1] == heads - 2:
                first = k - heads // 2 + 1
                finish(steps[k][0], g, [heard.pop(m) for m in range(first, k + 1)])

    if groups == 1:
        several(range(width), 0)
    else:

        def one(index, carry):
            several([index // groups], index % groups)
            return carry

        lax.fori_loop(0, width * groups, one, 0)
    for s in range(parts):
        at = (hop(s, parts) ^ me ^ over(col, 2)) * (cols * width)
        at = pl.ds(pl.multiple_of(at, cols * width), cols * width)
        outs[s][...] = update[at, :].astype(BF).reshape(cols, width, chans)


def place_kernel(parts, *refs):
    out_ref, wide = refs[2 * parts :]
    rows, cols, chans = out_ref.shape
    width = cols // parts
    me = lax.axis_index("row")
    odd = lax.axis_index("col") & 1
    step = min(rows // 2, 16)

    def body(index, carry):
        low = pl.multiple_of(index * step, step)
        for side in range(2):
            for s in range(parts):
                first = pl.multiple_of((me ^ hop(s, parts)) * width, width)
                piece = refs[side * parts + s][pl.ds(low, step)]
                wide[side, pl.ds(low, step), pl.ds(first, width), :] = piece.astype(F32)
            at = pl.multiple_of((odd ^ side) * (rows // 2) + low, step)
            out_ref[pl.ds(at, step)] = wide[side, pl.ds(low, step)].astype(BF)
        return carry

    lax.fori_loop(0, rows // 2 // step, body, 0, unroll=rows <= 64)


def per_device(
    pair, token_mask, ln_gain, ln_shift, w_qkv, w_bias, w_gate, gate_bias, w_out, out_bias
):
    rows, cols, chans = pair.shape
    heads = w_bias.shape[1]
    inner = w_gate.shape[1]
    parts = lax.axis_size("row")
    col_count = lax.axis_size("col")
    count = rows * parts
    width = cols // parts
    lanes = heads * cols
    vmem = pl.BlockSpec(memory_space=pltpu.VMEM)
    hbm = pl.BlockSpec(memory_space=pltpu.HBM)
    large = count > 256
    params = pltpu.CompilerParams(vmem_limit_bytes=VMEM_LIMIT if large else VMEM_LIMIT // 4)
    alone = pltpu.CompilerParams(vmem_limit_bytes=VMEM_ALONE)

    def swap(x, axis, offset):
        size = lax.axis_size(axis)
        return lax.ppermute(x, axis, [(i, i ^ offset) for i in range(size)])

    layers = lanes // chans
    first_rows = rows // 4
    parcels = pl.pallas_call(
        prep_kernel,
        out_shape=[jax.ShapeDtypeStruct((first_rows * width + rows * layers, chans), BF)] * parts
        + [jax.ShapeDtypeStruct(((rows - first_rows) * width, chans), BF)] * parts,
        in_specs=[hbm] * 4,
        out_specs=[vmem] * (2 * parts),
        scratch_shapes=[
            pltpu.VMEM((rows, cols, chans), BF),
            pltpu.VMEM((1, chans), F32),
            pltpu.VMEM((1, chans), F32),
            pltpu.VMEM((heads, chans), BF),
            pltpu.VMEM((rows, cols, chans), F32),
            pltpu.SemaphoreType.DMA((5,)),
        ],
        compiler_params=alone,
        name="prep",
    )(pair, ln_gain.reshape(1, chans), ln_shift.reshape(1, chans), w_bias.T)

    span = (128 // cols) * lanes
    shared = pl.pallas_call(
        functools.partial(constants_kernel, parts, cols, lanes),
        out_shape=[
            jax.ShapeDtypeStruct((chans, 4 * inner), BF),
            jax.ShapeDtypeStruct((1, inner), F32),
            jax.ShapeDtypeStruct((inner, chans), BF),
            jax.ShapeDtypeStruct((1, chans), F32),
            jax.ShapeDtypeStruct((span, span), BF),
            jax.ShapeDtypeStruct((count, 128), F32),
        ],
        in_specs=[hbm] * 6,
        out_specs=[vmem] * 6,
        scratch_shapes=[
            pltpu.VMEM((1, count), jnp.int32),
            pltpu.VMEM((count, 128), F32),
            pltpu.SemaphoreType.DMA((6,)),
        ],
        cost_estimate=pl.CostEstimate(
            flops=span * span * 8, bytes_accessed=span * span * 2, transcendentals=0
        ),
        compiler_params=params,
        name="constants",
    )(
        token_mask.reshape(1, count),
        w_qkv,
        w_gate,
        gate_bias.reshape(1, inner),
        w_out,
        out_bias.reshape(1, chans),
    )

    def back(pieces):
        return [pieces[0]] + [swap(pieces[s], "row", hop(s, parts)) for s in range(1, parts)]

    early = back(parcels[:parts])
    shared, *waiting = lax.optimization_barrier((shared, *parcels[parts:]))
    late = back(waiting)

    def project(pieces, size):
        tokens = parts * size
        batch = max(1, 256 // tokens)
        return pl.pallas_call(
            functools.partial(project_kernel, parts, (inner // heads) ** (-0.5), size),
            out_shape=[jax.ShapeDtypeStruct((width, tokens, inner), BF)] * 3
            + [jax.ShapeDtypeStruct((width, tokens, inner), F32)],
            in_specs=[vmem] * (parts + 2),
            out_specs=[vmem] * 4,
            scratch_shapes=[
                pltpu.VMEM((parts, size * width, chans), F32),
                pltpu.VMEM((width // batch, tokens * batch, chans), BF),
            ],
            cost_estimate=pl.CostEstimate(
                flops=8 * width * tokens * chans * inner,
                bytes_accessed=width * tokens * (2 * chans + 10 * inner),
                transcendentals=width * tokens * inner,
            ),
            compiler_params=params,
            name="project",
        )(*pieces, weight, gate_row)

    by_row = jnp.stack([p[first_rows * width :].reshape(layers, rows, chans) for p in early])
    weight, gate_row, *shared = shared
    from_chips = [swap(by_row, "col", 2 * t) for t in range(1, col_count // 2)]
    first = project(early, first_rows)
    second = project(late, rows - first_rows)
    from_chips, second = lax.optimization_barrier((from_chips, second))
    by_chip = jnp.stack([by_row] + from_chips)
    other = swap(by_chip, "col", 1)

    block = jax.ShapeDtypeStruct((cols, width, chans), BF)

    def attend(side, tiles):
        return pl.pallas_call(
            functools.partial(attend_kernel, parts, side),
            out_shape=[block] * parts,
            in_specs=[vmem] * 13,
            out_specs=[vmem] * parts,
            scratch_shapes=[
                pltpu.VMEM((count // 2 * width, chans), F32),
                pltpu.VMEM((count // 256, count, heads * 128), F32),
            ],
            cost_estimate=pl.CostEstimate(
                flops=4 * width * count * count * inner,
                bytes_accessed=width * count * 8 * inner,
                transcendentals=width * heads * count * count // 2,
            ),
            compiler_params=params,
            name="attend",
        )(*first, *second, tiles, *shared)

    same = back(attend(0, by_chip))
    crossed = back(attend(1, other))
    return pl.pallas_call(
        functools.partial(place_kernel, parts),
        out_shape=jax.ShapeDtypeStruct((rows, cols, chans), BF),
        in_specs=[vmem] * (2 * parts),
        out_specs=vmem,
        scratch_shapes=[pltpu.VMEM((2, rows // 2, cols, chans), F32)],
        compiler_params=params,
        name="place",
    )(*same, *crossed)


def solution(mesh):
    in_specs = (P("row", "col", None), P(), P(), P(), P(), P(), P(), P(), P(), P())
    out_specs = P("row", "col", None)
    return jax.shard_map(
        per_device, mesh=mesh, in_specs=in_specs, out_specs=out_specs, check_vma=False
    )
```

```python
import functools

import jax
import jax.numpy as jnp
from jax import lax
from jax.experimental import pallas as pl
from jax.experimental.pallas import tpu as pltpu
from jax.sharding import PartitionSpec as P

BF = jnp.bfloat16
F32 = jnp.float32
VMEM_LIMIT = 52 * 1024 * 1024
VMEM_ALONE = 62 * 1024 * 1024


def dot(a, b):
    return jnp.dot(a, b, preferred_element_type=F32)


def dot_t(a, b):
    return lax.dot_general(a, b, (((1,), (1,)), ((), ())), preferred_element_type=F32)


def dot_l(a, b):
    return lax.dot_general(a, b, (((0,), (0,)), ((), ())), preferred_element_type=F32)


def over(a, size):
    return lax.shift_right_logical(a, jnp.full_like(a, size.bit_length() - 1))


def below(a, size):
    return a & (size - 1)


def hop(s, parts):
    return (parts - s) & (parts - 1)


def column_of(row, width):
    return jnp.broadcast_to(row, (width, row.shape[1])).T


def split_sum(a, ones):
    first = a.astype(BF)
    rest = a - first.astype(F32)
    second = rest.astype(BF)
    third = (rest - second.astype(F32)).astype(BF)
    return dot(first, ones) + dot(second, ones) + dot(third, ones)


def pipelined(count, stages, lags):
    kept = {}
    for turn in range(count + max(lags)):
        for k, (stage, lag) in enumerate(zip(stages, lags)):
            if 0 <= turn - lag < count:
                given = kept.pop((k - 1, turn - lag), ())
                kept[k, turn - lag] = stage(turn - lag, *given)


def prep_kernel(pair_ref, gain_ref, shift_ref, wb_ref, *refs):
    outs, (raw, gain, shift, wbt, wide, early, late, sem, sent) = refs[:-9], refs[-9:]
    parts = len(outs) // 2
    parcels = [early.at[s] for s in range(parts)] + [late.at[s] for s in range(parts)]
    rows, cols, chans = pair_ref.shape
    heads = wb_ref.shape[0]
    lanes = heads * cols
    width = cols // parts
    me = lax.axis_index("row")
    step = min(rows, 16)
    half = rows // 2
    first_rows = rows // 4
    small = [
        pltpu.make_async_copy(source, target, sem.at[n])
        for n, (source, target) in enumerate(((wb_ref, wbt), (gain_ref, gain), (shift_ref, shift)))
    ]
    for copy in small:
        copy.start()

    fetches = [
        pltpu.make_async_copy(
            pair_ref.at[pl.ds(n * half, half)], raw.at[pl.ds(n * half, half)], sem.at[3 + n]
        )
        for n in range(2)
    ]
    for copy in fetches:
        copy.start()
    ones = jnp.ones((chans, chans), BF)
    lane_col = below(lax.broadcasted_iota(jnp.int32, (cols, lanes), 1), cols)
    keep = lane_col == lax.broadcasted_iota(jnp.int32, (cols, lanes), 0)
    head_of = over(lax.broadcasted_iota(jnp.int32, (lanes, heads), 0), cols)
    spread = (head_of == lax.broadcasted_iota(jnp.int32, (lanes, heads), 1)).astype(BF)
    for copy in small:
        copy.wait()
    wb = dot(spread, wbt[...]).astype(BF)

    def centre(start):
        values = raw[pl.ds(start, step)].reshape(step * cols, chans)
        mean = dot(values, ones) * (1.0 / chans)
        centred = values.astype(F32) - mean
        return centred, split_sum(centred * centred, ones) * (1.0 / chans)

    def scale(start, centred, var):
        normed = (centred * lax.rsqrt(var + 1e-05) * gain[...] + shift[...]).astype(BF)
        return normed, dot_t(normed, wb)

    def store(start, which, normed, every):
        every = every.reshape(step, cols, lanes)
        tile = jnp.sum(jnp.where(keep[None], every, 0.0), axis=1).astype(BF)
        wide[pl.ds(start, step)] = normed.astype(F32).reshape(step, cols, chans)
        to = pl.multiple_of((start - which * first_rows) * width, step * width)
        to = pl.ds(to, step * width)
        for s in range(parts):
            first = pl.multiple_of((me ^ hop(s, parts)) * width, width)
            chunk = wide[pl.ds(start, step), pl.ds(first, width), :].reshape(step * width, chans)
            parcels[which * parts + s][to, :] = chunk.astype(BF)
            for layer in range(lanes // chans):
                row = pl.multiple_of(first_rows * width + rows * layer + start, step)
                parcels[s][pl.ds(row, step), :] = tile[:, layer * chans : (layer + 1) * chans]
        return ()

    leaving = []

    def leave(n, low, size):
        for s in range(n * parts, (n + 1) * parts):
            at = pl.ds(low, size)
            copy = pltpu.make_async_copy(parcels[s].at[at], outs[s].at[at], sent.at[len(leaving)])
            copy.start()
            leaving.append(copy)

    if rows <= 64:

        def first_stage(n):
            if n * step in (0, half):
                fetches[n * step // half].wait()
            return centre(n * step)

        def second_stage(n, centred, var):
            return scale(n * step, centred, var)

        def third_stage(n, normed, every):
            which = int(n * step >= first_rows)
            store(n * step, which, normed, every)
            leave(which, (n * step - which * first_rows) * width, step * width)
            return ()

        pipelined(rows // step, (first_stage, second_stage, third_stage), (0, 1, 2))
    else:
        for copy in fetches:
            copy.wait()
        for low, high, which in ((0, first_rows, 0), (first_rows, rows, 1)):

            def one(index, carry, low=low, which=which):
                start = pl.multiple_of(low + index * step, step)
                store(start, which, *scale(start, *centre(start)))
                return carry

            lax.fori_loop(0, (high - low) // step, one, 0)
            leave(which, 0, (high - low) * width)
    leave(0, first_rows * width, rows * (lanes // chans))
    for copy in leaving:
        copy.wait()


def project_kernel(parts, scale, size, *refs):
    parcels = refs[:parts]
    weight, gate_bias, q_ref, k_ref, v_ref, gate_ref, wide, tokens = refs[parts:]
    width, count, inner = q_ref.shape
    batch = tokens.shape[1] // count
    me = lax.axis_index("row")
    for s in range(parts):
        wide[s] = parcels[s][0 : size * width, :].astype(F32)

    def lay(j):
        for k in range(batch):
            for s in range(parts):
                at = pl.multiple_of(k * count + (me ^ hop(s, parts)) * size, size)
                line = wide[s, pl.ds(batch * j + k, size, stride=width), :]
                tokens[j, pl.ds(at, size), :] = line.astype(BF)
        return ()

    def multiply(j):
        return (dot(tokens[j], weight[...]),)

    def store(j, mixed):
        query = (mixed[:, 0:inner] * scale).astype(BF)
        gate = jax.nn.sigmoid(mixed[:, 3 * inner : 4 * inner] + gate_bias[...])
        for k in range(batch):
            at = slice(k * count, (k + 1) * count)
            q_ref[batch * j + k] = query[at]
            k_ref[batch * j + k] = mixed[at, inner : 2 * inner].astype(BF)
            v_ref[batch * j + k] = mixed[at, 2 * inner : 3 * inner].astype(BF)
            gate_ref[batch * j + k] = gate[at]
        return ()

    if count <= 256:
        pipelined(width // batch, (lay, multiply, store), (0, 1, 2))
    else:

        def one(j, carry):
            lay(j)
            store(j, *multiply(j))
            return carry

        lax.fori_loop(0, width // batch, one, 0)


def constants_kernel(parts, cols, lanes, *refs):
    mask_ref, wqkv_ref, wg_ref, gb_ref, wo_ref, ob_ref = refs[:6]
    weight_ref, gate_ref, out_ref, base_ref, order_ref, key_ref, mask, scratch, sem = refs[6:]
    inner = wg_ref.shape[1]
    moves = (
        (mask_ref, mask),
        (wqkv_ref, weight_ref.at[:, pl.ds(0, 3 * inner)]),
        (wg_ref, weight_ref.at[:, pl.ds(3 * inner, inner)]),
        (gb_ref, gate_ref),
        (wo_ref, out_ref),
        (ob_ref, base_ref),
    )
    copies = [
        pltpu.make_async_copy(source, target, sem.at[n])
        for n, (source, target) in enumerate(moves)
    ]
    for copy in copies:
        copy.start()
    span = order_ref.shape[0]
    source_lane = lax.broadcasted_iota(jnp.int32, (span, span), 0)
    target_lane = lax.broadcasted_iota(jnp.int32, (span, span), 1)
    tile_of, rest = over(source_lane, lanes), below(source_lane, lanes)
    wanted = over(rest, cols) * 128 + tile_of * cols + below(rest, cols)
    order_ref[...] = (wanted == target_lane).astype(BF)
    for copy in copies:
        copy.wait()
    scratch[...] = jnp.where(column_of(mask[...], 128) == 1, 0.0, -1000000000.0).astype(F32)
    rows = key_ref.shape[0] // parts
    first_rows = rows // 4
    to = 0
    for low, high in ((0, first_rows), (first_rows, rows)):
        for p in range(parts):
            key_ref[to : to + high - low] = scratch[p * rows + low : p * rows + high]
            to += high - low


def attend_kernel(parts, side, *refs):
    halves = refs[0:4], refs[4:8]
    tiles, out_weight, out_bias, order_ref, key_ref = refs[8:13]
    outs = refs[13 : parts + 13]
    update, bias = refs[parts + 13 :]
    width, early, inner = halves[0][0].shape
    count = early + halves[1][0].shape[1]
    first_rows = early // parts
    pairs, _, layers, rows, chans = tiles.shape
    groups = bias.shape[0]
    heads = bias.shape[2] // 128
    lanes = layers * chans
    cols = lanes // heads
    head = inner // heads
    me = lax.axis_index("row")
    col = lax.axis_index("col")
    group = 128 // cols
    batch = max(1, min(count, 256) // rows)

    def one_block(index, carry):
        g, b = index // (parts // batch), index % (parts // batch)
        block = jnp.concatenate(
            [
                tiles[g * group + t, pl.ds(b * batch, batch), n].reshape(batch * rows, chans)
                for t in range(group)
                for n in range(layers)
            ],
            axis=1,
        )
        ordered = dot(block, order_ref[...])
        for s in range(batch):
            level = me ^ hop(b * batch + s, parts)
            for low, high, base in ((0, first_rows, 0), (first_rows, rows, early)):
                at = pl.multiple_of(base + level * (high - low), first_rows)
                at = pl.ds(at, high - low)
                some = slice(s * rows + low, s * rows + high)
                for h in range(heads):
                    across = slice(h * 128, (h + 1) * 128)
                    bias[g, at, across] = ordered[some, across] + key_ref[at, :]
        return carry

    blocks = groups * (parts // batch)
    lax.fori_loop(0, blocks, one_block, 0, unroll=blocks <= 2)

    lane_head = over(lax.broadcasted_iota(jnp.int32, (1, inner), 1), head)
    odd = (col & 1) ^ side

    def query_rows(j, g, n):
        found = []
        for t in range(group):
            level = over(col, 2) ^ hop(g * group + t, parts)
            base = level * (rows - first_rows)
            spots = (0, level * first_rows), (1, base + first_rows), (1, base + odd * 2 * first_rows)
            upper, lower, last = (
                halves[k][n][j, pl.ds(pl.multiple_of(at, first_rows), first_rows), :]
                for k, at in spots
            )
            found += [jnp.where(odd == 1, lower, upper), last]
        return jnp.concatenate(found, axis=0)

    def key_rows(j, n):
        return jnp.concatenate([halves[0][n][j], halves[1][n][j]], axis=0)

    def scores_of(j, g, h):
        query = query_rows(j, g, 0)
        blank = jnp.zeros_like(query)
        pair = [jnp.where(lane_head == n, query, blank) for n in (h, h + 1)]
        product = dot_t(key_rows(j, 1), jnp.concatenate(pair, axis=0))
        return product + bias[g, :, h * 128 : (h + 2) * 128]

    def weights_of(scores):
        top = jnp.max(scores, axis=0, keepdims=True)
        expo = jnp.exp(scores - top)
        total = jnp.sum(expo, axis=0, keepdims=True)
        return (expo * (1.0 / total)).astype(BF)

    def finish(j, g, heard):
        attended = jnp.zeros((128, inner), F32)
        for n in range(heads):
            part = heard[n // 2][n % 2 * 128 : (n % 2 + 1) * 128]
            attended = jnp.where(lane_head == n, part, attended)
        gated = (query_rows(j, g, 3) * attended.astype(BF).astype(F32)).astype(BF)
        result = dot(gated, out_weight[...]) + out_bias[...]
        update[pl.ds(g * 128 * width + j, 128, stride=width), :] = result

    def several(columns, g):
        steps = [(j, h) for j in columns for h in range(0, heads, 2)]
        scores = scores_of(steps[0][0], g, steps[0][1])
        total_steps = len(steps)
        scores, weights, heard = {}, {}, {}
        for n in range(-3, total_steps + 2 + 2):
            if 0 <= n + 3 < total_steps:
                j, h = steps[n + 3]
                scores[n + 3] = scores_of(j, g, h)
            if 0 <= n < total_steps:
                weights[n] = weights_of(scores.pop(n))
            k = n - 2
            if 0 <= k < total_steps:
                heard[k] = dot_l(weights.pop(k), key_rows(steps[k][0], 2))
            k = n - 2 - 2
            if 0 <= k < total_steps and steps[k][1] == heads - 2:
                first = k - heads // 2 + 1
                finish(steps[k][0], g, [heard.pop(m) for m in range(first, k + 1)])

    if groups == 1:
        several(range(width), 0)
    else:

        def one(index, carry):
            several([index // groups], index % groups)
            return carry

        lax.fori_loop(0, width * groups, one, 0)
    for s in range(parts):
        at = hop(hop(s, parts) ^ me ^ over(col, 2), parts) * (cols * width)
        at = pl.ds(pl.multiple_of(at, cols * width), cols * width)
        outs[s][...] = update[at, :].astype(BF).reshape(cols, width, chans)


def place_kernel(parts, *refs):
    out_ref, wide, result, sem = refs[2 * parts :]
    rows, cols, chans = out_ref.shape
    width = cols // parts
    me = lax.axis_index("row")
    odd = lax.axis_index("col") & 1
    step = min(rows // 2, 16)
    copies = []
    for side in range(2):
        for low in range(0, rows // 2, step):
            lines = slice(low, low + step)
            for s in range(parts):
                first = pl.multiple_of((me ^ hop(s, parts)) * width, width)
                piece = refs[(1 - side) * parts + s][lines]
                wide[side, lines, pl.ds(first, width), :] = piece.astype(F32)
            result[side, lines] = wide[side, lines].astype(BF)
            at = pl.multiple_of((odd ^ side) * (rows // 2) + low, step)
            copy = pltpu.make_async_copy(
                result.at[side, pl.ds(low, step)], out_ref.at[pl.ds(at, step)], sem.at[len(copies)]
            )
            copy.start()
            copies.append(copy)
    for copy in copies:
        copy.wait()


def per_device(
    pair, token_mask, ln_gain, ln_shift, w_qkv, w_bias, w_gate, gate_bias, w_out, out_bias
):
    rows, cols, chans = pair.shape
    heads = w_bias.shape[1]
    inner = w_gate.shape[1]
    parts = lax.axis_size("row")
    col_count = lax.axis_size("col")
    count = rows * parts
    width = cols // parts
    lanes = heads * cols
    vmem = pl.BlockSpec(memory_space=pltpu.VMEM)
    hbm = pl.BlockSpec(memory_space=pltpu.HBM)
    large = count > 256
    params = pltpu.CompilerParams(vmem_limit_bytes=VMEM_LIMIT if large else VMEM_LIMIT // 4)
    alone = pltpu.CompilerParams(vmem_limit_bytes=VMEM_ALONE)

    def swap(x, axis, offset):
        size = lax.axis_size(axis)
        return lax.ppermute(x, axis, [(i, i ^ offset) for i in range(size)])

    layers = lanes // chans
    first_rows = rows // 4
    early = first_rows * width + rows * layers, chans
    late = (rows - first_rows) * width, chans
    parcels = pl.pallas_call(
        prep_kernel,
        out_shape=[jax.ShapeDtypeStruct(early, BF)] * parts
        + [jax.ShapeDtypeStruct(late, BF)] * parts,
        in_specs=[hbm] * 4,
        out_specs=[hbm] * (2 * parts),
        scratch_shapes=[
            pltpu.VMEM((rows, cols, chans), BF),
            pltpu.VMEM((1, chans), F32),
            pltpu.VMEM((1, chans), F32),
            pltpu.VMEM((heads, chans), BF),
            pltpu.VMEM((rows, cols, chans), F32),
            pltpu.VMEM((parts, *early), BF),
            pltpu.VMEM((parts, *late), BF),
            pltpu.SemaphoreType.DMA((5,)),
            pltpu.SemaphoreType.DMA((parts * (rows // min(rows, 16) + 1),)),
        ],
        compiler_params=alone,
        name="prep",
    )(pair, ln_gain.reshape(1, chans), ln_shift.reshape(1, chans), w_bias.T)

    span = (128 // cols) * lanes
    shared = pl.pallas_call(
        functools.partial(constants_kernel, parts, cols, lanes),
        out_shape=[
            jax.ShapeDtypeStruct((chans, 4 * inner), BF),
            jax.ShapeDtypeStruct((1, inner), F32),
            jax.ShapeDtypeStruct((inner, chans), BF),
            jax.ShapeDtypeStruct((1, chans), F32),
            jax.ShapeDtypeStruct((span, span), BF),
            jax.ShapeDtypeStruct((count, 128), F32),
        ],
        in_specs=[hbm] * 6,
        out_specs=[vmem] * 6,
        scratch_shapes=[
            pltpu.VMEM((1, count), jnp.int32),
            pltpu.VMEM((count, 128), F32),
            pltpu.SemaphoreType.DMA((6,)),
        ],
        cost_estimate=pl.CostEstimate(
            flops=span * span * 8, bytes_accessed=span * span * 2, transcendentals=0
        ),
        compiler_params=params,
        name="constants",
    )(
        token_mask.reshape(1, count),
        w_qkv,
        w_gate,
        gate_bias.reshape(1, inner),
        w_out,
        out_bias.reshape(1, chans),
    )

    def back(pieces):
        return [pieces[0]] + [swap(pieces[s], "row", hop(s, parts)) for s in range(1, parts)]

    early = back(parcels[:parts])
    shared, *waiting = lax.optimization_barrier((shared, *parcels[parts:]))
    late = back(waiting)

    def project(pieces, size):
        tokens = parts * size
        batch = max(1, 256 // tokens)
        return pl.pallas_call(
            functools.partial(project_kernel, parts, (inner // heads) ** (-0.5), size),
            out_shape=[jax.ShapeDtypeStruct((width, tokens, inner), BF)] * 3
            + [jax.ShapeDtypeStruct((width, tokens, inner), F32)],
            in_specs=[vmem] * (parts + 2),
            out_specs=[vmem] * 4,
            scratch_shapes=[
                pltpu.VMEM((parts, size * width, chans), F32),
                pltpu.VMEM((width // batch, tokens * batch, chans), BF),
            ],
            cost_estimate=pl.CostEstimate(
                flops=8 * width * tokens * chans * inner,
                bytes_accessed=width * tokens * (2 * chans + 10 * inner),
                transcendentals=width * tokens * inner,
            ),
            compiler_params=params,
            name="project",
        )(*pieces, weight, gate_row)

    by_row = jnp.stack([p[first_rows * width :].reshape(layers, rows, chans) for p in early])
    weight, gate_row, *shared = shared
    from_chips = [swap(by_row, "col", 2 * hop(t, parts)) for t in range(1, parts)]
    first = project(early, first_rows)
    late[0], first = lax.optimization_barrier((late[0], first))
    second = project(late, rows - first_rows)
    from_chips, second = lax.optimization_barrier((from_chips, second))
    by_chip = jnp.stack([by_row] + from_chips)
    other = swap(by_chip, "col", 1)

    block = jax.ShapeDtypeStruct((cols, width, chans), BF)

    def attend(side, tiles):
        return pl.pallas_call(
            functools.partial(attend_kernel, parts, side),
            out_shape=[block] * parts,
            in_specs=[vmem] * 13,
            out_specs=[vmem] * parts,
            scratch_shapes=[
                pltpu.VMEM((count // 2 * width, chans), F32),
                pltpu.VMEM((count // 256, count, heads * 128), F32),
            ],
            cost_estimate=pl.CostEstimate(
                flops=4 * width * count * count * inner,
                bytes_accessed=width * count * 8 * inner,
                transcendentals=width * heads * count * count // 2,
            ),
            compiler_params=params,
            name="attend",
        )(*first, *second, tiles, *shared)

    same = back(attend(0, by_chip))
    crossed = back(attend(1, other))
    return pl.pallas_call(
        functools.partial(place_kernel, parts),
        out_shape=jax.ShapeDtypeStruct((rows, cols, chans), BF),
        in_specs=[vmem] * (2 * parts),
        out_specs=hbm,
        scratch_shapes=[
            pltpu.VMEM((2, rows // 2, cols, chans), F32),
            pltpu.VMEM((2, rows // 2, cols, chans), BF),
            pltpu.SemaphoreType.DMA((2 * (rows // 2 // min(rows // 2, 16)),)),
        ],
        compiler_params=params,
        name="place",
    )(*crossed, *same)


def solution(mesh):
    in_specs = (P("row", "col", None), P(), P(), P(), P(), P(), P(), P(), P(), P())
    out_specs = P("row", "col", None)
    return jax.shard_map(
        per_device, mesh=mesh, in_specs=in_specs, out_specs=out_specs, check_vma=False
    )
```

```python
import functools

import jax
import jax.numpy as jnp
from jax import lax
from jax.experimental import pallas as pl
from jax.experimental.pallas import tpu as pltpu
from jax.sharding import PartitionSpec as P

BF = jnp.bfloat16
F32 = jnp.float32
VMEM_LIMIT = 52 * 1024 * 1024
VMEM_ALONE = 62 * 1024 * 1024


def dot(a, b):
    return jnp.dot(a, b, preferred_element_type=F32)


def dot_t(a, b):
    return lax.dot_general(a, b, (((1,), (1,)), ((), ())), preferred_element_type=F32)


def dot_l(a, b):
    return lax.dot_general(a, b, (((0,), (0,)), ((), ())), preferred_element_type=F32)


def over(a, size):
    return lax.shift_right_logical(a, jnp.full_like(a, size.bit_length() - 1))


def below(a, size):
    return a & (size - 1)


def hop(s, parts):
    return (parts - s) & (parts - 1)


def column_of(row, width):
    return jnp.broadcast_to(row, (width, row.shape[1])).T


def split_sum(a, ones):
    first = a.astype(BF)
    rest = a - first.astype(F32)
    second = rest.astype(BF)
    third = (rest - second.astype(F32)).astype(BF)
    return dot(first, ones) + dot(second, ones) + dot(third, ones)


def pipelined(count, stages, lags):
    kept = {}
    for turn in range(count + max(lags)):
        for k, (stage, lag) in enumerate(zip(stages, lags)):
            if 0 <= turn - lag < count:
                given = kept.pop((k - 1, turn - lag), ())
                kept[k, turn - lag] = stage(turn - lag, *given)


def prep_kernel(pair_ref, gain_ref, shift_ref, wb_ref, *refs):
    outs, (raw, gain, shift, wbt, wide, early, late, sem, sent) = refs[:-9], refs[-9:]
    parts = len(outs) // 2
    parcels = [early.at[s] for s in range(parts)] + [late.at[s] for s in range(parts)]
    rows, cols, chans = pair_ref.shape
    heads = wb_ref.shape[0]
    lanes = heads * cols
    width = cols // parts
    me = lax.axis_index("row")
    step = min(rows, 16)
    half = rows // 2
    first_rows = rows // 4
    small = [
        pltpu.make_async_copy(source, target, sem.at[n])
        for n, (source, target) in enumerate(((wb_ref, wbt), (gain_ref, gain), (shift_ref, shift)))
    ]
    for copy in small:
        copy.start()

    fetches = [
        pltpu.make_async_copy(
            pair_ref.at[pl.ds(n * half, half)], raw.at[pl.ds(n * half, half)], sem.at[3 + n]
        )
        for n in range(2)
    ]
    for copy in fetches:
        copy.start()
    ones = jnp.ones((chans, chans), BF)
    lane_col = below(lax.broadcasted_iota(jnp.int32, (cols, lanes), 1), cols)
    keep = lane_col == lax.broadcasted_iota(jnp.int32, (cols, lanes), 0)
    head_of = over(lax.broadcasted_iota(jnp.int32, (lanes, heads), 0), cols)
    spread = (head_of == lax.broadcasted_iota(jnp.int32, (lanes, heads), 1)).astype(BF)
    for copy in small:
        copy.wait()
    wb = dot(spread, wbt[...]).astype(BF)

    def centre(start):
        values = raw[pl.ds(start, step)].reshape(step * cols, chans)
        mean = dot(values, ones) * (1.0 / chans)
        centred = values.astype(F32) - mean
        return centred, split_sum(centred * centred, ones) * (1.0 / chans)

    def scale(start, centred, var):
        normed = (centred * lax.rsqrt(var + 1e-05) * gain[...] + shift[...]).astype(BF)
        return normed, dot_t(normed, wb)

    def store(start, which, normed, every):
        every = every.reshape(step, cols, lanes)
        tile = jnp.sum(jnp.where(keep[None], every, 0.0), axis=1).astype(BF)
        wide[pl.ds(start, step)] = normed.astype(F32).reshape(step, cols, chans)
        to = pl.multiple_of((start - which * first_rows) * width, step * width)
        to = pl.ds(to, step * width)
        for s in range(parts):
            first = pl.multiple_of((me ^ hop(s, parts)) * width, width)
            chunk = wide[pl.ds(start, step), pl.ds(first, width), :].reshape(step * width, chans)
            parcels[which * parts + s][to, :] = chunk.astype(BF)
            for layer in range(lanes // chans):
                row = pl.multiple_of(first_rows * width + rows * layer + start, step)
                parcels[s][pl.ds(row, step), :] = tile[:, layer * chans : (layer + 1) * chans]
        return ()

    leaving = []

    def leave(n, low, size):
        for s in range(n * parts, (n + 1) * parts):
            at = pl.ds(low, size)
            copy = pltpu.make_async_copy(parcels[s].at[at], outs[s].at[at], sent.at[len(leaving)])
            copy.start()
            leaving.append(copy)

    if rows <= 64:

        def first_stage(n):
            if n * step in (0, half):
                fetches[n * step // half].wait()
            return centre(n * step)

        def second_stage(n, centred, var):
            return scale(n * step, centred, var)

        def third_stage(n, normed, every):
            which = int(n * step >= first_rows)
            store(n * step, which, normed, every)
            leave(which, (n * step - which * first_rows) * width, step * width)
            return ()

        pipelined(rows // step, (first_stage, second_stage, third_stage), (0, 1, 2))
    else:
        for copy in fetches:
            copy.wait()
        for low, high, which in ((0, first_rows, 0), (first_rows, rows, 1)):

            def one(index, carry, low=low, which=which):
                start = pl.multiple_of(low + index * step, step)
                store(start, which, *scale(start, *centre(start)))
                return carry

            lax.fori_loop(0, (high - low) // step, one, 0)
            leave(which, 0, (high - low) * width)
    leave(0, first_rows * width, rows * (lanes // chans))
    for copy in leaving:
        copy.wait()


def project_kernel(parts, scale, size, *refs):
    parcels = refs[:parts]
    weight, gate_bias, q_ref, k_ref, v_ref, gate_ref, wide, tokens = refs[parts:]
    width, count, inner = q_ref.shape
    batch = tokens.shape[1] // count
    for s in range(parts):
        wide[s] = parcels[s][0 : size * width, :].astype(F32)

    def lay(j):
        for k in range(batch):
            for s in range(parts):
                line = wide[s, pl.ds(batch * j + k, size, stride=width), :]
                tokens[j, pl.ds(k * count + s * size, size), :] = line.astype(BF)
        return ()

    def multiply(j):
        return (dot(tokens[j], weight[...]),)

    def store(j, mixed):
        query = (mixed[:, 0:inner] * scale).astype(BF)
        gate = jax.nn.sigmoid(mixed[:, 3 * inner : 4 * inner] + gate_bias[...])
        for k in range(batch):
            at = slice(k * count, (k + 1) * count)
            q_ref[batch * j + k] = query[at]
            k_ref[batch * j + k] = mixed[at, inner : 2 * inner].astype(BF)
            v_ref[batch * j + k] = mixed[at, 2 * inner : 3 * inner].astype(BF)
            gate_ref[batch * j + k] = gate[at]
        return ()

    if count <= 256:
        pipelined(width // batch, (lay, multiply, store), (0, 1, 2))
    else:

        def one(j, carry):
            lay(j)
            store(j, *multiply(j))
            return carry

        lax.fori_loop(0, width // batch, one, 0)


def constants_kernel(parts, cols, lanes, *refs):
    mask_ref, wqkv_ref, wg_ref, gb_ref, wo_ref, ob_ref = refs[:6]
    weight_ref, gate_ref, out_ref, base_ref, order_ref, key_ref, mask, scratch, sem = refs[6:]
    inner = wg_ref.shape[1]
    moves = (
        (mask_ref, mask),
        (wqkv_ref, weight_ref.at[:, pl.ds(0, 3 * inner)]),
        (wg_ref, weight_ref.at[:, pl.ds(3 * inner, inner)]),
        (gb_ref, gate_ref),
        (wo_ref, out_ref),
        (ob_ref, base_ref),
    )
    copies = [
        pltpu.make_async_copy(source, target, sem.at[n])
        for n, (source, target) in enumerate(moves)
    ]
    for copy in copies:
        copy.start()
    span = order_ref.shape[0]
    source_lane = lax.broadcasted_iota(jnp.int32, (span, span), 0)
    target_lane = lax.broadcasted_iota(jnp.int32, (span, span), 1)
    tile_of, rest = over(source_lane, lanes), below(source_lane, lanes)
    wanted = over(rest, cols) * 128 + tile_of * cols + below(rest, cols)
    order_ref[...] = (wanted == target_lane).astype(BF)
    for copy in copies:
        copy.wait()
    scratch[...] = jnp.where(column_of(mask[...], 128) == 1, 0.0, -1000000000.0).astype(F32)
    rows = key_ref.shape[0] // parts
    first_rows = rows // 4
    to = 0
    for low, high in ((0, first_rows), (first_rows, rows)):
        for p in range(parts):
            key_ref[to : to + high - low] = scratch[p * rows + low : p * rows + high]
            to += high - low


def attend_kernel(parts, side, *refs):
    halves = refs[0:4], refs[4:8]
    tiles, out_weight, out_bias, order_ref, key_ref = refs[8:13]
    outs = refs[13 : parts + 13]
    update, bias = refs[parts + 13 :]
    width, early, inner = halves[0][0].shape
    count = early + halves[1][0].shape[1]
    first_rows = early // parts
    pairs, _, layers, rows, chans = tiles.shape
    groups = bias.shape[0]
    heads = bias.shape[2] // 128
    lanes = layers * chans
    cols = lanes // heads
    head = inner // heads
    me = lax.axis_index("row")
    col = lax.axis_index("col")
    group = 128 // cols
    batch = max(1, min(count, 256) // rows)

    def one_block(index, carry):
        g, b = index // (parts // batch), index % (parts // batch)
        block = jnp.concatenate(
            [
                tiles[g * group + t, pl.ds(b * batch, batch), n].reshape(batch * rows, chans)
                for t in range(group)
                for n in range(layers)
            ],
            axis=1,
        )
        ordered = dot(block, order_ref[...])
        for s in range(batch):
            place = b * batch + s
            level = me ^ hop(place, parts)
            for low, high, base in ((0, first_rows, 0), (first_rows, rows, early)):
                size = high - low
                key = key_ref[pl.ds(pl.multiple_of(base + level * size, first_rows), size), :]
                at = pl.ds(pl.multiple_of(base + place * size, first_rows), size)
                some = slice(s * rows + low, s * rows + high)
                for h in range(heads):
                    across = slice(h * 128, (h + 1) * 128)
                    bias[g, at, across] = ordered[some, across] + key
        return carry

    blocks = groups * (parts // batch)
    lax.fori_loop(0, blocks, one_block, 0, unroll=blocks <= 2)

    lane_head = over(lax.broadcasted_iota(jnp.int32, (1, inner), 1), head)
    odd = (col & 1) ^ side

    def query_rows(j, g, n):
        found = []
        for t in range(group):
            place = hop(me ^ over(col, 2) ^ hop(g * group + t, parts), parts)
            base = place * (rows - first_rows)
            spots = (0, place * first_rows), (1, base + first_rows), (1, base + odd * 2 * first_rows)
            upper, lower, last = (
                halves[k][n][j, pl.ds(pl.multiple_of(at, first_rows), first_rows), :]
                for k, at in spots
            )
            found += [jnp.where(odd == 1, lower, upper), last]
        return jnp.concatenate(found, axis=0)

    def key_rows(j, n):
        return jnp.concatenate([halves[0][n][j], halves[1][n][j]], axis=0)

    def scores_of(j, g, h):
        query = query_rows(j, g, 0)
        blank = jnp.zeros_like(query)
        pair = [jnp.where(lane_head == n, query, blank) for n in (h, h + 1)]
        product = dot_t(key_rows(j, 1), jnp.concatenate(pair, axis=0))
        return product + bias[g, :, h * 128 : (h + 2) * 128]

    def weights_of(scores):
        top = jnp.max(scores, axis=0, keepdims=True)
        expo = jnp.exp(scores - top)
        total = jnp.sum(expo, axis=0, keepdims=True)
        return (expo * (1.0 / total)).astype(BF)

    def finish(j, g, heard):
        attended = jnp.zeros((128, inner), F32)
        for n in range(heads):
            part = heard[n // 2][n % 2 * 128 : (n % 2 + 1) * 128]
            attended = jnp.where(lane_head == n, part, attended)
        gated = (query_rows(j, g, 3) * attended.astype(BF).astype(F32)).astype(BF)
        result = dot(gated, out_weight[...]) + out_bias[...]
        update[pl.ds(g * 128 * width + j, 128, stride=width), :] = result

    def several(columns, g):
        steps = [(j, h) for j in columns for h in range(0, heads, 2)]
        scores = scores_of(steps[0][0], g, steps[0][1])
        total_steps = len(steps)
        scores, weights, heard = {}, {}, {}
        for n in range(-3, total_steps + 2 + 2):
            if 0 <= n + 3 < total_steps:
                j, h = steps[n + 3]
                scores[n + 3] = scores_of(j, g, h)
            if 0 <= n < total_steps:
                weights[n] = weights_of(scores.pop(n))
            k = n - 2
            if 0 <= k < total_steps:
                heard[k] = dot_l(weights.pop(k), key_rows(steps[k][0], 2))
            k = n - 2 - 2
            if 0 <= k < total_steps and steps[k][1] == heads - 2:
                first = k - heads // 2 + 1
                finish(steps[k][0], g, [heard.pop(m) for m in range(first, k + 1)])

    if groups == 1:
        several(range(width), 0)
    else:

        def one(index, carry):
            several([index // groups], index % groups)
            return carry

        lax.fori_loop(0, width * groups, one, 0)
    for s in range(parts):
        at = hop(hop(s, parts) ^ me ^ over(col, 2), parts) * (cols * width)
        at = pl.ds(pl.multiple_of(at, cols * width), cols * width)
        outs[s][...] = update[at, :].astype(BF).reshape(cols, width, chans)


def place_kernel(parts, *refs):
    out_ref, wide, result, sem = refs[2 * parts :]
    rows, cols, chans = out_ref.shape
    width = cols // parts
    me = lax.axis_index("row")
    odd = lax.axis_index("col") & 1
    step = min(rows // 2, 16)
    copies = []
    for side in range(2):
        for low in range(0, rows // 2, step):
            lines = slice(low, low + step)
            for s in range(parts):
                first = pl.multiple_of((me ^ hop(s, parts)) * width, width)
                piece = refs[(1 - side) * parts + s][lines]
                wide[side, lines, pl.ds(first, width), :] = piece.astype(F32)
            result[side, lines] = wide[side, lines].astype(BF)
            at = pl.multiple_of((odd ^ side) * (rows // 2) + low, step)
            copy = pltpu.make_async_copy(
                result.at[side, pl.ds(low, step)], out_ref.at[pl.ds(at, step)], sem.at[len(copies)]
            )
            copy.start()
            copies.append(copy)
    for copy in copies:
        copy.wait()


def per_device(
    pair, token_mask, ln_gain, ln_shift, w_qkv, w_bias, w_gate, gate_bias, w_out, out_bias
):
    rows, cols, chans = pair.shape
    heads = w_bias.shape[1]
    inner = w_gate.shape[1]
    parts = lax.axis_size("row")
    col_count = lax.axis_size("col")
    count = rows * parts
    width = cols // parts
    lanes = heads * cols
    vmem = pl.BlockSpec(memory_space=pltpu.VMEM)
    hbm = pl.BlockSpec(memory_space=pltpu.HBM)
    large = count > 256
    params = pltpu.CompilerParams(vmem_limit_bytes=VMEM_LIMIT if large else VMEM_LIMIT // 4)
    alone = pltpu.CompilerParams(vmem_limit_bytes=VMEM_ALONE)

    def swap(x, axis, offset):
        size = lax.axis_size(axis)
        return lax.ppermute(x, axis, [(i, i ^ offset) for i in range(size)])

    layers = lanes // chans
    first_rows = rows // 4
    early = first_rows * width + rows * layers, chans
    late = (rows - first_rows) * width, chans
    parcels = pl.pallas_call(
        prep_kernel,
        out_shape=[jax.ShapeDtypeStruct(early, BF)] * parts
        + [jax.ShapeDtypeStruct(late, BF)] * parts,
        in_specs=[hbm] * 4,
        out_specs=[hbm] * (2 * parts),
        scratch_shapes=[
            pltpu.VMEM((rows, cols, chans), BF),
            pltpu.VMEM((1, chans), F32),
            pltpu.VMEM((1, chans), F32),
            pltpu.VMEM((heads, chans), BF),
            pltpu.VMEM((rows, cols, chans), F32),
            pltpu.VMEM((parts, *early), BF),
            pltpu.VMEM((parts, *late), BF),
            pltpu.SemaphoreType.DMA((5,)),
            pltpu.SemaphoreType.DMA((parts * (rows // min(rows, 16) + 1),)),
        ],
        compiler_params=alone,
        name="prep",
    )(pair, ln_gain.reshape(1, chans), ln_shift.reshape(1, chans), w_bias.T)

    span = (128 // cols) * lanes
    shared = pl.pallas_call(
        functools.partial(constants_kernel, parts, cols, lanes),
        out_shape=[
            jax.ShapeDtypeStruct((chans, 4 * inner), BF),
            jax.ShapeDtypeStruct((1, inner), F32),
            jax.ShapeDtypeStruct((inner, chans), BF),
            jax.ShapeDtypeStruct((1, chans), F32),
            jax.ShapeDtypeStruct((span, span), BF),
            jax.ShapeDtypeStruct((count, 128), F32),
        ],
        in_specs=[hbm] * 6,
        out_specs=[vmem] * 6,
        scratch_shapes=[
            pltpu.VMEM((1, count), jnp.int32),
            pltpu.VMEM((count, 128), F32),
            pltpu.SemaphoreType.DMA((6,)),
        ],
        cost_estimate=pl.CostEstimate(
            flops=span * span * 8, bytes_accessed=span * span * 2, transcendentals=0
        ),
        compiler_params=params,
        name="constants",
    )(
        token_mask.reshape(1, count),
        w_qkv,
        w_gate,
        gate_bias.reshape(1, inner),
        w_out,
        out_bias.reshape(1, chans),
    )

    def back(pieces):
        return [pieces[0]] + [swap(pieces[s], "row", hop(s, parts)) for s in range(1, parts)]

    early = back(parcels[:parts])
    shared, *waiting = lax.optimization_barrier((shared, *parcels[parts:]))
    late = back(waiting)

    def project(pieces, size):
        tokens = parts * size
        batch = max(1, 256 // tokens)
        return pl.pallas_call(
            functools.partial(project_kernel, parts, (inner // heads) ** (-0.5), size),
            out_shape=[jax.ShapeDtypeStruct((width, tokens, inner), BF)] * 3
            + [jax.ShapeDtypeStruct((width, tokens, inner), F32)],
            in_specs=[vmem] * (parts + 2),
            out_specs=[vmem] * 4,
            scratch_shapes=[
                pltpu.VMEM((parts, size * width, chans), F32),
                pltpu.VMEM((width // batch, tokens * batch, chans), BF),
            ],
            cost_estimate=pl.CostEstimate(
                flops=8 * width * tokens * chans * inner,
                bytes_accessed=width * tokens * (2 * chans + 10 * inner),
                transcendentals=width * tokens * inner,
            ),
            compiler_params=params,
            name="project",
        )(*pieces, weight, gate_row)

    by_row = jnp.stack([p[first_rows * width :].reshape(layers, rows, chans) for p in early])
    weight, gate_row, *shared = shared
    from_chips = [swap(by_row, "col", 2 * hop(t, parts)) for t in range(1, parts)]
    first = project(early, first_rows)
    late[0], first = lax.optimization_barrier((late[0], first))
    second = project(late, rows - first_rows)
    from_chips, second = lax.optimization_barrier((from_chips, second))
    by_chip = jnp.stack([by_row] + from_chips)
    other = swap(by_chip, "col", 1)

    block = jax.ShapeDtypeStruct((cols, width, chans), BF)

    def attend(side, tiles):
        return pl.pallas_call(
            functools.partial(attend_kernel, parts, side),
            out_shape=[block] * parts,
            in_specs=[vmem] * 13,
            out_specs=[vmem] * parts,
            scratch_shapes=[
                pltpu.VMEM((count // 2 * width, chans), F32),
                pltpu.VMEM((count // 256, count, heads * 128), F32),
            ],
            cost_estimate=pl.CostEstimate(
                flops=4 * width * count * count * inner,
                bytes_accessed=width * count * 8 * inner,
                transcendentals=width * heads * count * count // 2,
            ),
            compiler_params=params,
            name="attend",
        )(*first, *second, tiles, *shared)

    same = back(attend(0, by_chip))
    crossed = back(attend(1, other))
    return pl.pallas_call(
        functools.partial(place_kernel, parts),
        out_shape=jax.ShapeDtypeStruct((rows, cols, chans), BF),
        in_specs=[vmem] * (2 * parts),
        out_specs=hbm,
        scratch_shapes=[
            pltpu.VMEM((2, rows // 2, cols, chans), F32),
            pltpu.VMEM((2, rows // 2, cols, chans), BF),
            pltpu.SemaphoreType.DMA((2 * (rows // 2 // min(rows // 2, 16)),)),
        ],
        compiler_params=params,
        name="place",
    )(*crossed, *same)


def solution(mesh):
    in_specs = (P("row", "col", None), P(), P(), P(), P(), P(), P(), P(), P(), P())
    out_specs = P("row", "col", None)
    return jax.shard_map(
        per_device, mesh=mesh, in_specs=in_specs, out_specs=out_specs, check_vma=False
    )
```

```python
import functools

import jax
import jax.numpy as jnp
from jax import lax
from jax.experimental import pallas as pl
from jax.experimental.pallas import tpu as pltpu
from jax.sharding import PartitionSpec as P

BF = jnp.bfloat16
F32 = jnp.float32
VMEM_LIMIT = 52 * 1024 * 1024
VMEM_ALONE = 62 * 1024 * 1024


def dot(a, b):
    return jnp.dot(a, b, preferred_element_type=F32)


def dot_t(a, b):
    return lax.dot_general(a, b, (((1,), (1,)), ((), ())), preferred_element_type=F32)


def dot_l(a, b):
    return lax.dot_general(a, b, (((0,), (0,)), ((), ())), preferred_element_type=F32)


def over(a, size):
    return lax.shift_right_logical(a, jnp.full_like(a, size.bit_length() - 1))


def below(a, size):
    return a & (size - 1)


def hop(s, parts):
    return (parts - s) & (parts - 1)


def column_of(row, width):
    return jnp.broadcast_to(row, (width, row.shape[1])).T


def split_sum(a, ones):
    first = a.astype(BF)
    rest = a - first.astype(F32)
    second = rest.astype(BF)
    third = (rest - second.astype(F32)).astype(BF)
    return dot(first, ones) + dot(second, ones) + dot(third, ones)


def pipelined(count, stages, lags):
    kept = {}
    for turn in range(count + max(lags)):
        for k, (stage, lag) in enumerate(zip(stages, lags)):
            if 0 <= turn - lag < count:
                given = kept.pop((k - 1, turn - lag), ())
                kept[k, turn - lag] = stage(turn - lag, *given)


def prep_kernel(pair_ref, gain_ref, shift_ref, wb_ref, *refs):
    outs, (raw, gain, shift, wbt, wide, early, late, sem, sent) = refs[:-9], refs[-9:]
    parts = len(outs) // 2
    parcels = [early.at[s] for s in range(parts)] + [late.at[s] for s in range(parts)]
    rows, cols, chans = pair_ref.shape
    heads = wb_ref.shape[0]
    lanes = heads * cols
    width = cols // parts
    me = lax.axis_index("row")
    step = min(rows, 16)
    half = rows // 2
    first_rows = rows // 4
    small = [
        pltpu.make_async_copy(source, target, sem.at[n])
        for n, (source, target) in enumerate(((wb_ref, wbt), (gain_ref, gain), (shift_ref, shift)))
    ]
    for copy in small:
        copy.start()

    fetches = [
        pltpu.make_async_copy(
            pair_ref.at[pl.ds(n * half, half)], raw.at[pl.ds(n * half, half)], sem.at[3 + n]
        )
        for n in range(2)
    ]
    for copy in fetches:
        copy.start()
    ones = jnp.ones((chans, chans), BF)
    lane_col = below(lax.broadcasted_iota(jnp.int32, (cols, lanes), 1), cols)
    keep = lane_col == lax.broadcasted_iota(jnp.int32, (cols, lanes), 0)
    head_of = over(lax.broadcasted_iota(jnp.int32, (lanes, heads), 0), cols)
    spread = (head_of == lax.broadcasted_iota(jnp.int32, (lanes, heads), 1)).astype(BF)
    for copy in small:
        copy.wait()
    wb = dot(spread, wbt[...]).astype(BF)

    def centre(start):
        values = raw[pl.ds(start, step)].reshape(step * cols, chans)
        mean = dot(values, ones) * (1.0 / chans)
        centred = values.astype(F32) - mean
        return centred, split_sum(centred * centred, ones) * (1.0 / chans)

    def scale(start, centred, var):
        normed = (centred * lax.rsqrt(var + 1e-05) * gain[...] + shift[...]).astype(BF)
        return normed, dot_t(normed, wb)

    def store(start, which, normed, every):
        every = every.reshape(step, cols, lanes)
        tile = jnp.sum(jnp.where(keep[None], every, 0.0), axis=1).astype(BF)
        wide[pl.ds(start, step)] = normed.astype(F32).reshape(step, cols, chans)
        to = pl.multiple_of((start - which * first_rows) * width, step * width)
        to = pl.ds(to, step * width)
        for s in range(parts):
            first = pl.multiple_of((me ^ hop(s, parts)) * width, width)
            chunk = wide[pl.ds(start, step), pl.ds(first, width), :].reshape(step * width, chans)
            parcels[which * parts + s][to, :] = chunk.astype(BF)
            for layer in range(lanes // chans):
                row = pl.multiple_of(first_rows * width + rows * layer + start, step)
                parcels[s][pl.ds(row, step), :] = tile[:, layer * chans : (layer + 1) * chans]
        return ()

    leaving = []

    def leave(n, low, size):
        for s in range(n * parts, (n + 1) * parts):
            at = pl.ds(low, size)
            copy = pltpu.make_async_copy(parcels[s].at[at], outs[s].at[at], sent.at[len(leaving)])
            copy.start()
            leaving.append(copy)

    if rows <= 64:

        def first_stage(n):
            if n == 0:
                for copy in fetches:
                    copy.wait()
            return centre(n * step)

        def second_stage(n, centred, var):
            return scale(n * step, centred, var)

        def third_stage(n, normed, every):
            which = int(n * step >= first_rows)
            store(n * step, which, normed, every)
            leave(which, (n * step - which * first_rows) * width, step * width)
            return ()

        pipelined(rows // step, (first_stage, second_stage, third_stage), (0, 1, 2))
    else:
        for copy in fetches:
            copy.wait()
        for low, high, which in ((0, first_rows, 0), (first_rows, rows, 1)):

            def one(index, carry, low=low, which=which):
                start = pl.multiple_of(low + index * step, step)
                store(start, which, *scale(start, *centre(start)))
                return carry

            lax.fori_loop(0, (high - low) // step, one, 0)
            leave(which, 0, (high - low) * width)
    leave(0, first_rows * width, rows * (lanes // chans))
    for copy in leaving:
        copy.wait()


def project_kernel(parts, scale, size, *refs):
    parcels = refs[:parts]
    weight, gate_bias, q_ref, k_ref, v_ref, gate_ref, wide, tokens = refs[parts:]
    width, count, inner = q_ref.shape
    batch = tokens.shape[1] // count
    for s in range(parts):
        wide[s] = parcels[s][0 : size * width, :].astype(F32)

    def lay(j):
        for k in range(batch):
            for s in range(parts):
                line = wide[s, pl.ds(batch * j + k, size, stride=width), :]
                tokens[j, pl.ds(k * count + s * size, size), :] = line.astype(BF)
        return ()

    def multiply(j):
        return (dot(tokens[j], weight[...]),)

    def store(j, mixed):
        query = (mixed[:, 0:inner] * scale).astype(BF)
        gate = jax.nn.sigmoid(mixed[:, 3 * inner : 4 * inner] + gate_bias[...])
        for k in range(batch):
            at = slice(k * count, (k + 1) * count)
            q_ref[batch * j + k] = query[at]
            k_ref[batch * j + k] = mixed[at, inner : 2 * inner].astype(BF)
            v_ref[batch * j + k] = mixed[at, 2 * inner : 3 * inner].astype(BF)
            gate_ref[batch * j + k] = gate[at]
        return ()

    if count <= 256:
        pipelined(width // batch, (lay, multiply, store), (0, 1, 2))
    else:

        def one(j, carry):
            lay(j)
            store(j, *multiply(j))
            return carry

        lax.fori_loop(0, width // batch, one, 0)


def constants_kernel(parts, cols, lanes, *refs):
    mask_ref, wqkv_ref, wg_ref, gb_ref, wo_ref, ob_ref = refs[:6]
    weight_ref, gate_ref, out_ref, base_ref, order_ref, key_ref, mask, scratch, sem = refs[6:]
    inner = wg_ref.shape[1]
    moves = (
        (mask_ref, mask),
        (wqkv_ref, weight_ref.at[:, pl.ds(0, 3 * inner)]),
        (wg_ref, weight_ref.at[:, pl.ds(3 * inner, inner)]),
        (gb_ref, gate_ref),
        (wo_ref, out_ref),
        (ob_ref, base_ref),
    )
    copies = [
        pltpu.make_async_copy(source, target, sem.at[n])
        for n, (source, target) in enumerate(moves)
    ]
    for copy in copies:
        copy.start()
    span = order_ref.shape[0]
    source_lane = lax.broadcasted_iota(jnp.int32, (span, span), 0)
    target_lane = lax.broadcasted_iota(jnp.int32, (span, span), 1)
    tile_of, rest = over(source_lane, lanes), below(source_lane, lanes)
    wanted = over(rest, cols) * 128 + tile_of * cols + below(rest, cols)
    order_ref[...] = (wanted == target_lane).astype(BF)
    for copy in copies:
        copy.wait()
    scratch[...] = jnp.where(column_of(mask[...], 128) == 1, 0.0, -1000000000.0).astype(F32)
    rows = key_ref.shape[0] // parts
    first_rows = rows // 4
    to = 0
    for low, high in ((0, first_rows), (first_rows, rows)):
        for p in range(parts):
            key_ref[to : to + high - low] = scratch[p * rows + low : p * rows + high]
            to += high - low


def attend_kernel(parts, side, *refs):
    halves = refs[0:4], refs[4:8]
    tiles, out_weight, out_bias, order_ref, key_ref = refs[8:13]
    outs = refs[13 : parts + 13]
    update, bias = refs[parts + 13 :]
    width, early, inner = halves[0][0].shape
    count = early + halves[1][0].shape[1]
    first_rows = early // parts
    pairs, _, layers, rows, chans = tiles.shape
    groups = bias.shape[0]
    heads = bias.shape[2] // 128
    lanes = layers * chans
    cols = lanes // heads
    head = inner // heads
    me = lax.axis_index("row")
    col = lax.axis_index("col")
    group = 128 // cols
    batch = max(1, min(count, 256) // rows)

    def one_block(index, carry):
        g, b = index // (parts // batch), index % (parts // batch)
        block = jnp.concatenate(
            [
                tiles[g * group + t, pl.ds(b * batch, batch), n].reshape(batch * rows, chans)
                for t in range(group)
                for n in range(layers)
            ],
            axis=1,
        )
        ordered = dot(block, order_ref[...])
        for s in range(batch):
            place = b * batch + s
            level = me ^ hop(place, parts)
            for low, high, base in ((0, first_rows, 0), (first_rows, rows, early)):
                size = high - low
                key = key_ref[pl.ds(pl.multiple_of(base + level * size, first_rows), size), :]
                at = pl.ds(pl.multiple_of(base + place * size, first_rows), size)
                some = slice(s * rows + low, s * rows + high)
                for h in range(heads):
                    across = slice(h * 128, (h + 1) * 128)
                    bias[g, at, across] = ordered[some, across] + key
        return carry

    blocks = groups * (parts // batch)
    lax.fori_loop(0, blocks, one_block, 0, unroll=blocks <= 2)

    lane_head = over(lax.broadcasted_iota(jnp.int32, (1, inner), 1), head)
    odd = (col & 1) ^ side

    def query_rows(j, g, n):
        found = []
        for t in range(group):
            place = hop(me ^ over(col, 2) ^ hop(g * group + t, parts), parts)
            base = place * (rows - first_rows)
            spots = (0, place * first_rows), (1, base + first_rows), (1, base + odd * 2 * first_rows)
            upper, lower, last = (
                halves[k][n][j, pl.ds(pl.multiple_of(at, first_rows), first_rows), :]
                for k, at in spots
            )
            found += [jnp.where(odd == 1, lower, upper), last]
        return jnp.concatenate(found, axis=0)

    def key_rows(j, n):
        return jnp.concatenate([halves[0][n][j], halves[1][n][j]], axis=0)

    def scores_of(j, g, h):
        query = query_rows(j, g, 0)
        blank = jnp.zeros_like(query)
        pair = [jnp.where(lane_head == n, query, blank) for n in (h, h + 1)]
        product = dot_t(key_rows(j, 1), jnp.concatenate(pair, axis=0))
        return product + bias[g, :, h * 128 : (h + 2) * 128]

    def weights_of(scores):
        top = jnp.max(scores, axis=0, keepdims=True)
        expo = jnp.exp(scores - top)
        total = jnp.sum(expo, axis=0, keepdims=True)
        return (expo * (1.0 / total)).astype(BF)

    def finish(j, g, heard):
        attended = jnp.zeros((128, inner), F32)
        for n in range(heads):
            part = heard[n // 2][n % 2 * 128 : (n % 2 + 1) * 128]
            attended = jnp.where(lane_head == n, part, attended)
        gated = (query_rows(j, g, 3) * attended.astype(BF).astype(F32)).astype(BF)
        result = dot(gated, out_weight[...]) + out_bias[...]
        update[pl.ds(g * 128 * width + j, 128, stride=width), :] = result

    def several(columns, g):
        steps = [(j, h) for j in columns for h in range(0, heads, 2)]
        scores = scores_of(steps[0][0], g, steps[0][1])
        total_steps = len(steps)
        scores, weights, heard = {}, {}, {}
        for n in range(-2, total_steps + 2 + 2):
            if 0 <= n + 2 < total_steps:
                j, h = steps[n + 2]
                scores[n + 2] = scores_of(j, g, h)
            if 0 <= n < total_steps:
                weights[n] = weights_of(scores.pop(n))
            k = n - 2
            if 0 <= k < total_steps:
                heard[k] = dot_l(weights.pop(k), key_rows(steps[k][0], 2))
            k = n - 2 - 2
            if 0 <= k < total_steps and steps[k][1] == heads - 2:
                first = k - heads // 2 + 1
                finish(steps[k][0], g, [heard.pop(m) for m in range(first, k + 1)])

    if groups == 1:
        several(range(width), 0)
    else:

        def one(index, carry):
            several([index // groups], index % groups)
            return carry

        lax.fori_loop(0, width * groups, one, 0)
    for s in range(parts):
        at = hop(hop(s, parts) ^ me ^ over(col, 2), parts) * (cols * width)
        at = pl.ds(pl.multiple_of(at, cols * width), cols * width)
        outs[s][...] = update[at, :].astype(BF).reshape(cols, width, chans)


def place_kernel(parts, *refs):
    out_ref, wide, result, sem = refs[2 * parts :]
    rows, cols, chans = out_ref.shape
    width = cols // parts
    me = lax.axis_index("row")
    odd = lax.axis_index("col") & 1
    step = min(rows // 2, 16)
    copies = []
    for side in range(2):
        for low in range(0, rows // 2, step):
            lines = slice(low, low + step)
            for s in range(parts):
                first = pl.multiple_of((me ^ hop(s, parts)) * width, width)
                piece = refs[(1 - side) * parts + s][lines]
                wide[side, lines, pl.ds(first, width), :] = piece.astype(F32)
            result[side, lines] = wide[side, lines].astype(BF)
            at = pl.multiple_of((odd ^ side) * (rows // 2) + low, step)
            copy = pltpu.make_async_copy(
                result.at[side, pl.ds(low, step)], out_ref.at[pl.ds(at, step)], sem.at[len(copies)]
            )
            copy.start()
            copies.append(copy)
    for copy in copies:
        copy.wait()


def per_device(
    pair, token_mask, ln_gain, ln_shift, w_qkv, w_bias, w_gate, gate_bias, w_out, out_bias
):
    rows, cols, chans = pair.shape
    heads = w_bias.shape[1]
    inner = w_gate.shape[1]
    parts = lax.axis_size("row")
    col_count = lax.axis_size("col")
    count = rows * parts
    width = cols // parts
    lanes = heads * cols
    vmem = pl.BlockSpec(memory_space=pltpu.VMEM)
    hbm = pl.BlockSpec(memory_space=pltpu.HBM)
    large = count > 256
    params = pltpu.CompilerParams(vmem_limit_bytes=VMEM_LIMIT if large else VMEM_LIMIT // 4)
    alone = pltpu.CompilerParams(vmem_limit_bytes=VMEM_ALONE)

    def swap(x, axis, offset):
        size = lax.axis_size(axis)
        return lax.ppermute(x, axis, [(i, i ^ offset) for i in range(size)])

    layers = lanes // chans
    first_rows = rows // 4
    early = first_rows * width + rows * layers, chans
    late = (rows - first_rows) * width, chans
    parcels = pl.pallas_call(
        prep_kernel,
        out_shape=[jax.ShapeDtypeStruct(early, BF)] * parts
        + [jax.ShapeDtypeStruct(late, BF)] * parts,
        in_specs=[hbm] * 4,
        out_specs=[hbm] * (2 * parts),
        scratch_shapes=[
            pltpu.VMEM((rows, cols, chans), BF),
            pltpu.VMEM((1, chans), F32),
            pltpu.VMEM((1, chans), F32),
            pltpu.VMEM((heads, chans), BF),
            pltpu.VMEM((rows, cols, chans), F32),
            pltpu.VMEM((parts, *early), BF),
            pltpu.VMEM((parts, *late), BF),
            pltpu.SemaphoreType.DMA((5,)),
            pltpu.SemaphoreType.DMA((parts * (rows // min(rows, 16) + 1),)),
        ],
        compiler_params=alone,
        name="prep",
    )(pair, ln_gain.reshape(1, chans), ln_shift.reshape(1, chans), w_bias.T)

    span = (128 // cols) * lanes
    shared = pl.pallas_call(
        functools.partial(constants_kernel, parts, cols, lanes),
        out_shape=[
            jax.ShapeDtypeStruct((chans, 4 * inner), BF),
            jax.ShapeDtypeStruct((1, inner), F32),
            jax.ShapeDtypeStruct((inner, chans), BF),
            jax.ShapeDtypeStruct((1, chans), F32),
            jax.ShapeDtypeStruct((span, span), BF),
            jax.ShapeDtypeStruct((count, 128), F32),
        ],
        in_specs=[hbm] * 6,
        out_specs=[vmem] * 6,
        scratch_shapes=[
            pltpu.VMEM((1, count), jnp.int32),
            pltpu.VMEM((count, 128), F32),
            pltpu.SemaphoreType.DMA((6,)),
        ],
        cost_estimate=pl.CostEstimate(
            flops=span * span * 8, bytes_accessed=span * span * 2, transcendentals=0
        ),
        compiler_params=params,
        name="constants",
    )(
        token_mask.reshape(1, count),
        w_qkv,
        w_gate,
        gate_bias.reshape(1, inner),
        w_out,
        out_bias.reshape(1, chans),
    )

    def back(pieces):
        return [pieces[0]] + [swap(pieces[s], "row", hop(s, parts)) for s in range(1, parts)]

    early = back(parcels[:parts])
    shared, *waiting = lax.optimization_barrier((shared, *parcels[parts:]))
    late = back(waiting)

    def project(pieces, size):
        tokens = parts * size
        batch = max(1, 256 // tokens)
        return pl.pallas_call(
            functools.partial(project_kernel, parts, (inner // heads) ** (-0.5), size),
            out_shape=[jax.ShapeDtypeStruct((width, tokens, inner), BF)] * 3
            + [jax.ShapeDtypeStruct((width, tokens, inner), F32)],
            in_specs=[vmem] * (parts + 2),
            out_specs=[vmem] * 4,
            scratch_shapes=[
                pltpu.VMEM((parts, size * width, chans), F32),
                pltpu.VMEM((width // batch, tokens * batch, chans), BF),
            ],
            cost_estimate=pl.CostEstimate(
                flops=8 * width * tokens * chans * inner,
                bytes_accessed=width * tokens * (2 * chans + 10 * inner),
                transcendentals=width * tokens * inner,
            ),
            compiler_params=params,
            name="project",
        )(*pieces, weight, gate_row)

    by_row = jnp.stack([p[first_rows * width :].reshape(layers, rows, chans) for p in early])
    weight, gate_row, *shared = shared
    from_chips = [swap(by_row, "col", 2 * hop(t, parts)) for t in range(1, parts)]
    first = project(early, first_rows)
    late[0], first = lax.optimization_barrier((late[0], first))
    second = project(late, rows - first_rows)
    from_chips, second = lax.optimization_barrier((from_chips, second))
    by_chip = jnp.stack([by_row] + from_chips)
    other = swap(by_chip, "col", 1)

    block = jax.ShapeDtypeStruct((cols, width, chans), BF)

    def attend(side, tiles):
        return pl.pallas_call(
            functools.partial(attend_kernel, parts, side),
            out_shape=[block] * parts,
            in_specs=[vmem] * 13,
            out_specs=[vmem] * parts,
            scratch_shapes=[
                pltpu.VMEM((count // 2 * width, chans), F32),
                pltpu.VMEM((count // 256, count, heads * 128), F32),
            ],
            cost_estimate=pl.CostEstimate(
                flops=4 * width * count * count * inner,
                bytes_accessed=width * count * 8 * inner,
                transcendentals=width * heads * count * count // 2,
            ),
            compiler_params=params,
            name="attend",
        )(*first, *second, tiles, *shared)

    same = back(attend(0, by_chip))
    crossed = back(attend(1, other))
    return pl.pallas_call(
        functools.partial(place_kernel, parts),
        out_shape=jax.ShapeDtypeStruct((rows, cols, chans), BF),
        in_specs=[vmem] * (2 * parts),
        out_specs=hbm,
        scratch_shapes=[
            pltpu.VMEM((2, rows // 2, cols, chans), F32),
            pltpu.VMEM((2, rows // 2, cols, chans), BF),
            pltpu.SemaphoreType.DMA((2 * (rows // 2 // min(rows // 2, 16)),)),
        ],
        compiler_params=params,
        name="place",
    )(*crossed, *same)


def solution(mesh):
    in_specs = (P("row", "col", None), P(), P(), P(), P(), P(), P(), P(), P(), P())
    out_specs = P("row", "col", None)
    return jax.shard_map(
        per_device, mesh=mesh, in_specs=in_specs, out_specs=out_specs, check_vma=False
    )
```

```python
import functools

import jax
import jax.numpy as jnp
from jax import lax
from jax.experimental import pallas as pl
from jax.experimental.pallas import tpu as pltpu
from jax.sharding import PartitionSpec as P

BF = jnp.bfloat16
F32 = jnp.float32
VMEM_LIMIT = 52 * 1024 * 1024
VMEM_ALONE = 62 * 1024 * 1024


def dot(a, b):
    return jnp.dot(a, b, preferred_element_type=F32)


def dot_t(a, b):
    return lax.dot_general(a, b, (((1,), (1,)), ((), ())), preferred_element_type=F32)


def dot_l(a, b):
    return lax.dot_general(a, b, (((0,), (0,)), ((), ())), preferred_element_type=F32)


def over(a, size):
    return lax.shift_right_logical(a, jnp.full_like(a, size.bit_length() - 1))


def below(a, size):
    return a & (size - 1)


def hop(s, parts):
    return (parts - s) & (parts - 1)


def column_of(row, width):
    return jnp.broadcast_to(row, (width, row.shape[1])).T


def split_sum(a, ones):
    first = a.astype(BF)
    rest = a - first.astype(F32)
    second = rest.astype(BF)
    third = (rest - second.astype(F32)).astype(BF)
    return dot(first, ones) + dot(second, ones) + dot(third, ones)


def pipelined(count, stages, lags):
    kept = {}
    for turn in range(count + max(lags)):
        for k, (stage, lag) in enumerate(zip(stages, lags)):
            if 0 <= turn - lag < count:
                given = kept.pop((k - 1, turn - lag), ())
                kept[k, turn - lag] = stage(turn - lag, *given)


def prep_kernel(pair_ref, gain_ref, shift_ref, wb_ref, *refs):
    outs, (raw, gain, shift, wbt, wide, early, late, sem, sent) = refs[:-9], refs[-9:]
    parts = len(outs) // 2
    parcels = [early.at[s] for s in range(parts)] + [late.at[s] for s in range(parts)]
    rows, cols, chans = pair_ref.shape
    heads = wb_ref.shape[0]
    lanes = heads * cols
    width = cols // parts
    me = lax.axis_index("row")
    step = min(rows, 16)
    half = rows // 2
    first_rows = rows // 4
    small = [
        pltpu.make_async_copy(source, target, sem.at[n])
        for n, (source, target) in enumerate(((wb_ref, wbt), (gain_ref, gain), (shift_ref, shift)))
    ]
    for copy in small:
        copy.start()

    fetches = [
        pltpu.make_async_copy(
            pair_ref.at[pl.ds(n * half, half)], raw.at[pl.ds(n * half, half)], sem.at[3 + n]
        )
        for n in range(2)
    ]
    for copy in fetches:
        copy.start()
    ones = jnp.ones((chans, chans), BF)
    lane_col = below(lax.broadcasted_iota(jnp.int32, (cols, lanes), 1), cols)
    keep = lane_col == lax.broadcasted_iota(jnp.int32, (cols, lanes), 0)
    head_of = over(lax.broadcasted_iota(jnp.int32, (lanes, heads), 0), cols)
    spread = (head_of == lax.broadcasted_iota(jnp.int32, (lanes, heads), 1)).astype(BF)
    for copy in small:
        copy.wait()
    wb = dot(spread, wbt[...]).astype(BF)

    def centre(start):
        values = raw[pl.ds(start, step)].reshape(step * cols, chans)
        mean = dot(values, ones) * (1.0 / chans)
        centred = values.astype(F32) - mean
        return centred, split_sum(centred * centred, ones) * (1.0 / chans)

    def scale(start, centred, var):
        normed = (centred * lax.rsqrt(var + 1e-05) * gain[...] + shift[...]).astype(BF)
        return normed, dot_t(normed, wb)

    def store(start, which, normed, every):
        every = every.reshape(step, cols, lanes)
        tile = jnp.sum(jnp.where(keep[None], every, 0.0), axis=1).astype(BF)
        wide[pl.ds(start, step)] = normed.astype(F32).reshape(step, cols, chans)
        to = pl.multiple_of((start - which * first_rows) * width, step * width)
        to = pl.ds(to, step * width)
        for s in range(parts):
            first = pl.multiple_of((me ^ hop(s, parts)) * width, width)
            chunk = wide[pl.ds(start, step), pl.ds(first, width), :].reshape(step * width, chans)
            parcels[which * parts + s][to, :] = chunk.astype(BF)
            for layer in range(lanes // chans):
                row = pl.multiple_of(first_rows * width + rows * layer + start, step)
                parcels[s][pl.ds(row, step), :] = tile[:, layer * chans : (layer + 1) * chans]
        return ()

    leaving = []

    def leave(n, low, size):
        for s in range(n * parts, (n + 1) * parts):
            at = pl.ds(low, size)
            copy = pltpu.make_async_copy(parcels[s].at[at], outs[s].at[at], sent.at[len(leaving)])
            copy.start()
            leaving.append(copy)

    if rows <= 64:

        def first_stage(n):
            if n * step in (0, half):
                fetches[n * step // half].wait()
            return centre(n * step)

        def second_stage(n, centred, var):
            return scale(n * step, centred, var)

        def third_stage(n, normed, every):
            which = int(n * step >= first_rows)
            store(n * step, which, normed, every)
            leave(which, (n * step - which * first_rows) * width, step * width)
            return ()

        pipelined(rows // step, (first_stage, second_stage, third_stage), (0, 1, 2))
    else:
        for copy in fetches:
            copy.wait()
        for low, high, which in ((0, first_rows, 0), (first_rows, rows, 1)):

            def one(index, carry, low=low, which=which):
                start = pl.multiple_of(low + index * step, step)
                store(start, which, *scale(start, *centre(start)))
                return carry

            lax.fori_loop(0, (high - low) // step, one, 0)
            leave(which, 0, (high - low) * width)
    leave(0, first_rows * width, rows * (lanes // chans))
    for copy in leaving:
        copy.wait()


def project_kernel(parts, scale, size, *refs):
    parcels = refs[:parts]
    weight, gate_bias, q_ref, k_ref, v_ref, gate_ref, wide, tokens = refs[parts:]
    width, count, inner = q_ref.shape
    batch = tokens.shape[1] // count
    for s in range(parts):
        wide[s] = parcels[s][0 : size * width, :].astype(F32)

    def lay(j):
        for k in range(batch):
            for s in range(parts):
                line = wide[s, pl.ds(batch * j + k, size, stride=width), :]
                tokens[j, pl.ds(k * count + s * size, size), :] = line.astype(BF)
        return ()

    def multiply(j):
        return (dot(tokens[j], weight[...]),)

    def store(j, mixed):
        query = (mixed[:, 0:inner] * scale).astype(BF)
        gate = jax.nn.sigmoid(mixed[:, 3 * inner : 4 * inner] + gate_bias[...])
        for k in range(batch):
            at = slice(k * count, (k + 1) * count)
            q_ref[batch * j + k] = query[at]
            k_ref[batch * j + k] = mixed[at, inner : 2 * inner].astype(BF)
            v_ref[batch * j + k] = mixed[at, 2 * inner : 3 * inner].astype(BF)
            gate_ref[batch * j + k] = gate[at]
        return ()

    if count <= 256:
        pipelined(width // batch, (lay, multiply, store), (0, 1, 2))
    else:

        def one(j, carry):
            lay(j)
            store(j, *multiply(j))
            return carry

        lax.fori_loop(0, width // batch, one, 0)


def constants_kernel(parts, cols, lanes, *refs):
    mask_ref, wqkv_ref, wg_ref, gb_ref, wo_ref, ob_ref = refs[:6]
    weight_ref, gate_ref, out_ref, base_ref, order_ref, key_ref, mask, scratch, sem = refs[6:]
    inner = wg_ref.shape[1]
    moves = (
        (mask_ref, mask),
        (wqkv_ref, weight_ref.at[:, pl.ds(0, 3 * inner)]),
        (wg_ref, weight_ref.at[:, pl.ds(3 * inner, inner)]),
        (gb_ref, gate_ref),
        (wo_ref, out_ref),
        (ob_ref, base_ref),
    )
    copies = [
        pltpu.make_async_copy(source, target, sem.at[n])
        for n, (source, target) in enumerate(moves)
    ]
    for copy in copies:
        copy.start()
    span = order_ref.shape[0]
    source_lane = lax.broadcasted_iota(jnp.int32, (span, span), 0)
    target_lane = lax.broadcasted_iota(jnp.int32, (span, span), 1)
    tile_of, rest = over(source_lane, lanes), below(source_lane, lanes)
    wanted = over(rest, cols) * 128 + tile_of * cols + below(rest, cols)
    order_ref[...] = (wanted == target_lane).astype(BF)
    for copy in copies:
        copy.wait()
    scratch[...] = jnp.where(column_of(mask[...], 128) == 1, 0.0, -1000000000.0).astype(F32)
    rows = key_ref.shape[0] // parts
    first_rows = rows // 4
    to = 0
    for low, high in ((0, first_rows), (first_rows, rows)):
        for p in range(parts):
            key_ref[to : to + high - low] = scratch[p * rows + low : p * rows + high]
            to += high - low


def attend_kernel(parts, side, *refs):
    halves = refs[0:4], refs[4:8]
    tiles, out_weight, out_bias, order_ref, key_ref = refs[8:13]
    outs = refs[13 : parts + 13]
    update, bias = refs[parts + 13 :]
    width, early, inner = halves[0][0].shape
    count = early + halves[1][0].shape[1]
    first_rows = early // parts
    pairs, _, layers, rows, chans = tiles.shape
    groups = bias.shape[0]
    heads = bias.shape[2] // 128
    lanes = layers * chans
    cols = lanes // heads
    head = inner // heads
    me = lax.axis_index("row")
    col = lax.axis_index("col")
    group = 128 // cols
    batch = max(1, min(count, 256) // rows)

    def one_block(index, carry):
        g, b = index // (parts // batch), index % (parts // batch)
        block = jnp.concatenate(
            [
                tiles[g * group + t, pl.ds(b * batch, batch), n].reshape(batch * rows, chans)
                for t in range(group)
                for n in range(layers)
            ],
            axis=1,
        )
        ordered = dot(block, order_ref[...])
        for s in range(batch):
            place = b * batch + s
            level = me ^ hop(place, parts)
            for low, high, base in ((0, first_rows, 0), (first_rows, rows, early)):
                size = high - low
                key = key_ref[pl.ds(pl.multiple_of(base + level * size, first_rows), size), :]
                at = pl.ds(pl.multiple_of(base + place * size, first_rows), size)
                some = slice(s * rows + low, s * rows + high)
                for h in range(heads):
                    across = slice(h * 128, (h + 1) * 128)
                    bias[g, at, across] = ordered[some, across] + key
        return carry

    blocks = groups * (parts // batch)
    lax.fori_loop(0, blocks, one_block, 0, unroll=blocks <= 2)

    lane_head = over(lax.broadcasted_iota(jnp.int32, (1, inner), 1), head)
    odd = (col & 1) ^ side

    def query_rows(j, g, n):
        found = []
        for t in range(group):
            place = hop(me ^ over(col, 2) ^ hop(g * group + t, parts), parts)
            base = place * (rows - first_rows)
            spots = (0, place * first_rows), (1, base + first_rows), (1, base + odd * 2 * first_rows)
            upper, lower, last = (
                halves[k][n][j, pl.ds(pl.multiple_of(at, first_rows), first_rows), :]
                for k, at in spots
            )
            found += [jnp.where(odd == 1, lower, upper), last]
        return jnp.concatenate(found, axis=0)

    def key_rows(j, n):
        return jnp.concatenate([halves[0][n][j], halves[1][n][j]], axis=0)

    def scores_of(j, g, h):
        query = query_rows(j, g, 0)
        blank = jnp.zeros_like(query)
        pair = [jnp.where(lane_head == n, query, blank) for n in (h, h + 1)]
        product = dot_t(key_rows(j, 1), jnp.concatenate(pair, axis=0))
        return product + bias[g, :, h * 128 : (h + 2) * 128]

    def weights_of(scores):
        top = jnp.max(scores, axis=0, keepdims=True)
        expo = jnp.exp(scores - top)
        total = jnp.sum(expo, axis=0, keepdims=True)
        return (expo * (1.0 / total)).astype(BF)

    def finish(j, g, heard):
        attended = jnp.zeros((128, inner), F32)
        for n in range(heads):
            part = heard[n // 2][n % 2 * 128 : (n % 2 + 1) * 128]
            attended = jnp.where(lane_head == n, part, attended)
        gated = (query_rows(j, g, 3) * attended.astype(BF).astype(F32)).astype(BF)
        result = dot(gated, out_weight[...]) + out_bias[...]
        update[pl.ds(g * 128 * width + j, 128, stride=width), :] = result

    def several(columns, g):
        steps = [(j, h) for j in columns for h in range(0, heads, 2)]
        scores = scores_of(steps[0][0], g, steps[0][1])
        total_steps = len(steps)
        scores, weights, heard = {}, {}, {}
        for n in range(-3, total_steps + 2 + 2):
            if 0 <= n + 3 < total_steps:
                j, h = steps[n + 3]
                scores[n + 3] = scores_of(j, g, h)
            if 0 <= n < total_steps:
                weights[n] = weights_of(scores.pop(n))
            k = n - 2
            if 0 <= k < total_steps:
                heard[k] = dot_l(weights.pop(k), key_rows(steps[k][0], 2))
            k = n - 2 - 2
            if 0 <= k < total_steps and steps[k][1] == heads - 2:
                first = k - heads // 2 + 1
                finish(steps[k][0], g, [heard.pop(m) for m in range(first, k + 1)])

    if groups == 1:
        several(range(width), 0)
    else:

        def one(index, carry):
            several([index // groups], index % groups)
            return carry

        lax.fori_loop(0, width * groups, one, 0)
    for s in range(parts):
        at = hop(hop(s, parts) ^ me ^ over(col, 2), parts) * (cols * width)
        at = pl.ds(pl.multiple_of(at, cols * width), cols * width)
        outs[s][...] = update[at, :].astype(BF).reshape(cols, width, chans)


def place_kernel(parts, *refs):
    out_ref, wide, result, sem = refs[2 * parts :]
    rows, cols, chans = out_ref.shape
    width = cols // parts
    me = lax.axis_index("row")
    odd = lax.axis_index("col") & 1
    step = min(rows // 2, 8)
    copies = []
    for side in range(2):
        for low in range(0, rows // 2, step):
            lines = slice(low, low + step)
            for s in range(parts):
                first = pl.multiple_of((me ^ hop(s, parts)) * width, width)
                piece = refs[(1 - side) * parts + s][lines]
                wide[side, lines, pl.ds(first, width), :] = piece.astype(F32)
            result[side, lines] = wide[side, lines].astype(BF)
            at = pl.multiple_of((odd ^ side) * (rows // 2) + low, step)
            copy = pltpu.make_async_copy(
                result.at[side, pl.ds(low, step)], out_ref.at[pl.ds(at, step)], sem.at[len(copies)]
            )
            copy.start()
            copies.append(copy)
    for copy in copies:
        copy.wait()


def per_device(
    pair, token_mask, ln_gain, ln_shift, w_qkv, w_bias, w_gate, gate_bias, w_out, out_bias
):
    rows, cols, chans = pair.shape
    heads = w_bias.shape[1]
    inner = w_gate.shape[1]
    parts = lax.axis_size("row")
    col_count = lax.axis_size("col")
    count = rows * parts
    width = cols // parts
    lanes = heads * cols
    vmem = pl.BlockSpec(memory_space=pltpu.VMEM)
    hbm = pl.BlockSpec(memory_space=pltpu.HBM)
    large = count > 256
    params = pltpu.CompilerParams(vmem_limit_bytes=VMEM_LIMIT if large else VMEM_LIMIT // 4)
    alone = pltpu.CompilerParams(vmem_limit_bytes=VMEM_ALONE)

    def swap(x, axis, offset):
        size = lax.axis_size(axis)
        return lax.ppermute(x, axis, [(i, i ^ offset) for i in range(size)])

    layers = lanes // chans
    first_rows = rows // 4
    early = first_rows * width + rows * layers, chans
    late = (rows - first_rows) * width, chans
    parcels = pl.pallas_call(
        prep_kernel,
        out_shape=[jax.ShapeDtypeStruct(early, BF)] * parts
        + [jax.ShapeDtypeStruct(late, BF)] * parts,
        in_specs=[hbm] * 4,
        out_specs=[hbm] * (2 * parts),
        scratch_shapes=[
            pltpu.VMEM((rows, cols, chans), BF),
            pltpu.VMEM((1, chans), F32),
            pltpu.VMEM((1, chans), F32),
            pltpu.VMEM((heads, chans), BF),
            pltpu.VMEM((rows, cols, chans), F32),
            pltpu.VMEM((parts, *early), BF),
            pltpu.VMEM((parts, *late), BF),
            pltpu.SemaphoreType.DMA((5,)),
            pltpu.SemaphoreType.DMA((parts * (rows // min(rows, 16) + 1),)),
        ],
        compiler_params=alone,
        name="prep",
    )(pair, ln_gain.reshape(1, chans), ln_shift.reshape(1, chans), w_bias.T)

    span = (128 // cols) * lanes
    shared = pl.pallas_call(
        functools.partial(constants_kernel, parts, cols, lanes),
        out_shape=[
            jax.ShapeDtypeStruct((chans, 4 * inner), BF),
            jax.ShapeDtypeStruct((1, inner), F32),
            jax.ShapeDtypeStruct((inner, chans), BF),
            jax.ShapeDtypeStruct((1, chans), F32),
            jax.ShapeDtypeStruct((span, span), BF),
            jax.ShapeDtypeStruct((count, 128), F32),
        ],
        in_specs=[hbm] * 6,
        out_specs=[vmem] * 6,
        scratch_shapes=[
            pltpu.VMEM((1, count), jnp.int32),
            pltpu.VMEM((count, 128), F32),
            pltpu.SemaphoreType.DMA((6,)),
        ],
        cost_estimate=pl.CostEstimate(
            flops=span * span * 8, bytes_accessed=span * span * 2, transcendentals=0
        ),
        compiler_params=params,
        name="constants",
    )(
        token_mask.reshape(1, count),
        w_qkv,
        w_gate,
        gate_bias.reshape(1, inner),
        w_out,
        out_bias.reshape(1, chans),
    )

    def back(pieces):
        return [pieces[0]] + [swap(pieces[s], "row", hop(s, parts)) for s in range(1, parts)]

    early = back(parcels[:parts])
    shared, *waiting = lax.optimization_barrier((shared, *parcels[parts:]))
    late = back(waiting)

    def project(pieces, size):
        tokens = parts * size
        batch = max(1, 256 // tokens)
        return pl.pallas_call(
            functools.partial(project_kernel, parts, (inner // heads) ** (-0.5), size),
            out_shape=[jax.ShapeDtypeStruct((width, tokens, inner), BF)] * 3
            + [jax.ShapeDtypeStruct((width, tokens, inner), F32)],
            in_specs=[vmem] * (parts + 2),
            out_specs=[vmem] * 4,
            scratch_shapes=[
                pltpu.VMEM((parts, size * width, chans), F32),
                pltpu.VMEM((width // batch, tokens * batch, chans), BF),
            ],
            cost_estimate=pl.CostEstimate(
                flops=8 * width * tokens * chans * inner,
                bytes_accessed=width * tokens * (2 * chans + 10 * inner),
                transcendentals=width * tokens * inner,
            ),
            compiler_params=params,
            name="project",
        )(*pieces, weight, gate_row)

    by_row = jnp.stack([p[first_rows * width :].reshape(layers, rows, chans) for p in early])
    weight, gate_row, *shared = shared
    from_chips = [swap(by_row, "col", 2 * hop(t, parts)) for t in range(1, parts)]
    first = project(early, first_rows)
    late[0], first = lax.optimization_barrier((late[0], first))
    second = project(late, rows - first_rows)
    from_chips, second = lax.optimization_barrier((from_chips, second))
    by_chip = jnp.stack([by_row] + from_chips)
    other = swap(by_chip, "col", 1)

    block = jax.ShapeDtypeStruct((cols, width, chans), BF)

    def attend(side, tiles):
        return pl.pallas_call(
            functools.partial(attend_kernel, parts, side),
            out_shape=[block] * parts,
            in_specs=[vmem] * 13,
            out_specs=[vmem] * parts,
            scratch_shapes=[
                pltpu.VMEM((count // 2 * width, chans), F32),
                pltpu.VMEM((count // 256, count, heads * 128), F32),
            ],
            cost_estimate=pl.CostEstimate(
                flops=4 * width * count * count * inner,
                bytes_accessed=width * count * 8 * inner,
                transcendentals=width * heads * count * count // 2,
            ),
            compiler_params=params,
            name="attend",
        )(*first, *second, tiles, *shared)

    same = back(attend(0, by_chip))
    crossed = back(attend(1, other))
    return pl.pallas_call(
        functools.partial(place_kernel, parts),
        out_shape=jax.ShapeDtypeStruct((rows, cols, chans), BF),
        in_specs=[vmem] * (2 * parts),
        out_specs=hbm,
        scratch_shapes=[
            pltpu.VMEM((2, rows // 2, cols, chans), F32),
            pltpu.VMEM((2, rows // 2, cols, chans), BF),
            pltpu.SemaphoreType.DMA((2 * (rows // 2 // min(rows // 2, 8)),)),
        ],
        compiler_params=params,
        name="place",
    )(*crossed, *same)


def solution(mesh):
    in_specs = (P("row", "col", None), P(), P(), P(), P(), P(), P(), P(), P(), P())
    out_specs = P("row", "col", None)
    return jax.shard_map(
        per_device, mesh=mesh, in_specs=in_specs, out_specs=out_specs, check_vma=False
    )
```
